256 devices in a mesh: space: 64 (over z, y_lo, x), chan: 4 (over y_hi, core).
Axes of the slice: x: 4, y: 4 (y_hi: 2, y_lo: 2; y = y_hi * 2 + y_lo), z: 8, core: 2. Of those that a mesh axis runs over, the one named last changes fastest.
Arguments:
- features: bfloat16 [4096, 32, 512], P(('space', 'chan')), may hold values from -6 to 6
- occupancy: int32 [4096], P(('space', 'chan')), may hold values 0 or 1
- neighbours: int32 [4096, 6], P(('space', 'chan')), may hold values from -1 to 4095, as said below
- conv_weight: bfloat16 [27, 32, 32], replicated, may hold values from -0.21875 to 0.21875
- conv_bias: float32 [32], replicated, may hold values from -3 to 3
- latent: bfloat16 [262144, 512], P(('space', 'chan')), may hold values from -6 to 6
- token_proj: bfloat16 [32, 512], replicated, may hold values from -1 to 1
- norm_gain: float32 [512], replicated, may hold values from 0.25 to 1.75
- qkv_weight: bfloat16 [3, 512, 512], replicated
- out_weight: bfloat16 [512, 512], replicated, may hold values from -0.25 to 0.25
Outputs:
- conv_out: bfloat16 [4096, 32, 512], P(('space', 'chan'))
- tokens_out: bfloat16 [512, 262144], P(None, ('space', 'chan'))
The draws below stay inside these ranges and needn't reach their ends.
Inputs may be any that keep to these rules, and one draw needn't show every extreme that they name: `neighbours`: entry [b, d] is the brick across face d of brick b (d = 0..5 for -x, +x, -y, +y, -z, +z), or -1 where there is none. Brick b lies on device b // 16 in the order of space+chan, and a neighbour lies on a device whose index differs from its brick's by at most 2.
All inputs are finite; a program needn't handle non-finite values. No bound on the sum of `occupancy` on one device may be relied on, other than what follows from the above.
Results may differ from the reference program's by a relative error of at most 0.0054.
Values may be sent and summed in bfloat16 or wider, within the bound.
A program may use at most 128 MiB of HBM per device.

```python
import jax
import jax.numpy as jnp
from jax import lax

C = 32
D = 512
HEADS = 8
HD = 64
WIN = 1024
REACH = 2
BR_DEV = 16
BRICKS = 4096
TOKENS = 262144
N_SPACE = 64
N_CHAN = 4


def draw_neighbours(key, part):
    key_offset, key_slot, key_keep = jax.random.split(key, 3)
    brick_ids = jnp.arange(BRICKS, dtype=jnp.int32)[:, None]
    owner = brick_ids // BR_DEV
    spread = jax.random.randint(key_offset, (BRICKS, 6), -REACH, REACH + 1)
    target = jnp.clip(owner + spread, 0, BRICKS // BR_DEV - 1)
    slots = jax.random.randint(key_slot, (BRICKS, 6), 0, BR_DEV)
    keep_draw = jax.random.randint(key_keep, (BRICKS, 6), 0, 8)
    linked = jnp.where(keep_draw < 7, target * BR_DEV + slots, -1)
    linked = linked.at[0, 0].set(-1)
    linked = linked.at[BRICKS - 2, 5].set(BRICKS - 1)
    return linked.astype(jnp.int32)


def draw_qkv_weight(key, part):
    key_q, key_k, key_v = jax.random.split(key, 3)
    scale_in = D ** (-0.5)
    query_part = jax.random.normal(key_q, (D, D), jnp.float32) * scale_in
    key_part = jax.random.normal(key_k, (D, D), jnp.float32) * scale_in
    value_part = jax.random.normal(key_v, (D, D), jnp.float32) * scale_in
    return jnp.stack([query_part, key_part, value_part]).astype(jnp.bfloat16)


def plant(values, stream_key, smallest, high):
    extent = values.shape
    place = [jax.random.randint(jax.random.fold_in(stream_key, axis), (), 0, extent[axis]) for axis in range(len(extent))]
    values = values.at[tuple(place)].set(smallest)
    longest = extent.index(max(extent))
    place[longest] = (place[longest] + 1) % extent[longest]
    return values.at[tuple(place)].set(high)


def steps_of(rng, dims, cuts, least, high):
    level = 1.0
    for dim, parts in cuts:
        draws = jax.random.uniform(jax.random.fold_in(jax.random.fold_in(rng, 6), dim), (parts,), jnp.float32, least / len(cuts), high / len(cuts))
        level = level * jnp.repeat(jnp.exp(draws), dims[dim] // parts).reshape((-1,) + (1,) * (len(dims) - 1 - dim))
    return level


def normal_values(stream_key, shape, width, reach, cuts=(), kind=jnp.bfloat16):
    array = width * jax.random.normal(stream_key, shape, jnp.float32)
    if cuts:
        array = array * steps_of(stream_key, shape, cuts, -0.22, 0.18)
    return jnp.clip(array, -reach, reach).astype(kind)


def setup_inputs(seed: int = 0) -> dict:
    key_of = jax.random.split(jax.random.key(seed), 11)
    return {
        "features": normal_values(key_of[0], (BRICKS, C, 512), 1.0, 6.0, ((0, 256),)),
        "occupancy": plant((jax.random.randint(key_of[1], (BRICKS,), 0, 4) < 3).astype(jnp.int32), jax.random.fold_in(key_of[1], 1), 0, 1),
        "neighbours": draw_neighbours(jax.random.fold_in(key_of[10], 71), 0),
        "conv_weight": normal_values(key_of[3], (27, C, C), (27 * C) ** -0.5, 0.21875),
        "conv_bias": normal_values(key_of[4], (C,), 0.5, 3.0, (), jnp.float32),
        "latent": normal_values(key_of[5], (TOKENS, D), 1.0, 6.0, ((0, 256),)),
        "token_proj": normal_values(key_of[6], (C, D), C ** -0.5, 1.0),
        "norm_gain": jnp.clip(1.0 + 0.15 * jax.random.normal(key_of[7], (D,), jnp.float32), 0.25, 1.75),
        "qkv_weight": draw_qkv_weight(jax.random.fold_in(key_of[10], 71), 0),
        "out_weight": normal_values(key_of[9], (D, D), D ** -0.5, 0.25),
    }


def face_table(voxels):
    brick_count, channels = (voxels.shape[0], voxels.shape[1])
    sheets = [voxels[:, :, 7, :, :], voxels[:, :, 0, :, :], voxels[:, :, :, 7, :], voxels[:, :, :, 0, :], voxels[:, :, :, :, 7], voxels[:, :, :, :, 0]]
    return jnp.stack([sheet.reshape(brick_count, channels, 64) for sheet in sheets], axis=1)

def extend(voxels, gathered):
    brick_count, channels = (voxels.shape[0], voxels.shape[1])
    sheets = gathered.reshape(brick_count, 6, channels, 8, 8)
    padded = jnp.pad(voxels, ((0, 0), (0, 0), (1, 1), (1, 1), (1, 1)))
    padded = padded.at[:, :, 0, 1:9, 1:9].set(sheets[:, 0])
    padded = padded.at[:, :, 9, 1:9, 1:9].set(sheets[:, 1])
    padded = padded.at[:, :, 1:9, 0, 1:9].set(sheets[:, 2])
    padded = padded.at[:, :, 1:9, 9, 1:9].set(sheets[:, 3])
    padded = padded.at[:, :, 1:9, 1:9, 0].set(sheets[:, 4])
    padded = padded.at[:, :, 1:9, 1:9, 9].set(sheets[:, 5])
    return padded

def convolve(padded, weight):
    brick_count, channels = (padded.shape[0], padded.shape[1])
    running = jnp.zeros((brick_count, weight.shape[1], 512), jnp.float32)
    for step_x in range(3):
        for step_y in range(3):
            for step_z in range(3):
                slab = padded[:, :, step_x:step_x + 8, step_y:step_y + 8, step_z:step_z + 8]
                slab = slab.reshape(brick_count, channels, 512).astype(jnp.float32)
                kernel_tap = weight[step_x * 9 + step_y * 3 + step_z].astype(jnp.float32)
                running = running + jnp.einsum('kc,bcv->bkv', kernel_tap, slab)
    return running

def pool_tokens(conv_out):
    brick_count, channels = (conv_out.shape[0], conv_out.shape[1])
    cells = conv_out.astype(jnp.float32).reshape(brick_count, channels, 2, 2, 2, 2, 2, 2, 2, 2, 2)
    means = lax.optimization_barrier(jnp.mean(cells, axis=(4, 7, 10)))
    means = jnp.transpose(means, (1, 0, 2, 4, 6, 3, 5, 7))
    return means.reshape(channels, brick_count * 64).astype(jnp.bfloat16)

def rms_norm(mixed_in, norm_gain):
    scale_row = lax.rsqrt(lax.optimization_barrier(jnp.mean(mixed_in * mixed_in, axis=-1, keepdims=True)) + 1e-06)
    return (mixed_in * scale_row * norm_gain[None, :]).astype(jnp.bfloat16)

def reference(features, occupancy, neighbours, conv_weight, conv_bias, latent, token_proj, norm_gain, qkv_weight, out_weight):
    alive = occupancy.astype(jnp.float32)
    masked = (features.astype(jnp.float32) * alive[:, None, None]).astype(jnp.bfloat16)
    voxels = masked.reshape(BRICKS, C, 8, 8, 8)
    faces = face_table(voxels).reshape(BRICKS * 6, C, 64)
    has_peer = neighbours >= 0
    face_index = jnp.where(has_peer, neighbours, 0) * 6 + jnp.arange(6, dtype=jnp.int32)[None, :]

    def per_block(first_row):
        block_vox = lax.dynamic_slice_in_dim(voxels, first_row, BR_DEV, 0)
        block_index = lax.dynamic_slice_in_dim(face_index, first_row, BR_DEV, 0)
        block_peer = lax.dynamic_slice_in_dim(has_peer, first_row, BR_DEV, 0)
        gathered = jnp.take(faces, block_index.reshape(-1), axis=0).reshape(BR_DEV, 6, C, 64)
        gathered = jnp.where(block_peer[:, :, None, None], gathered, jnp.zeros_like(gathered))
        summed = convolve(extend(block_vox, gathered), conv_weight)
        own_part = lax.dynamic_slice_in_dim(masked, first_row, BR_DEV, 0).astype(jnp.float32)
        block_alive = lax.dynamic_slice_in_dim(alive, first_row, BR_DEV, 0)
        mixed = own_part + jax.nn.silu(summed + conv_bias[None, :, None])
        return (block_alive[:, None, None] * mixed).astype(jnp.bfloat16)
    starts = jnp.arange(N_SPACE * N_CHAN, dtype=jnp.int32) * BR_DEV
    conv_out = lax.map(per_block, starts).reshape(BRICKS, C, 512)
    pooled = pool_tokens(conv_out)
    mixed_in = latent.astype(jnp.float32) + jnp.dot(pooled.T, token_proj, preferred_element_type=jnp.float32)
    normed = rms_norm(mixed_in, norm_gain)
    queries = jnp.dot(normed, qkv_weight[0], preferred_element_type=jnp.float32).astype(jnp.bfloat16)
    keys = jnp.dot(normed, qkv_weight[1], preferred_element_type=jnp.float32).astype(jnp.bfloat16)
    values = jnp.dot(normed, qkv_weight[2], preferred_element_type=jnp.float32).astype(jnp.bfloat16)
    token_alive = jnp.broadcast_to(occupancy[:, None], (BRICKS, 64)).reshape(TOKENS)
    half_win = WIN // 2
    window_count = TOKENS // WIN
    rolled_q = jnp.roll(queries, -half_win, axis=0).reshape(window_count, WIN, HEADS, HD)
    rolled_k = jnp.roll(keys, -half_win, axis=0).reshape(window_count, WIN, HEADS, HD)
    rolled_v = jnp.roll(values, -half_win, axis=0).reshape(window_count, WIN, HEADS, HD)
    rolled_alive = jnp.roll(token_alive, -half_win).reshape(window_count, WIN)
    diagonal = jnp.eye(WIN, dtype=bool)

    def per_window(inputs):
        win_q, win_k, win_v, win_alive = inputs
        scores = jnp.einsum('qhd,khd->hqk', win_q.astype(jnp.float32), win_k.astype(jnp.float32)) * HD ** (-0.5)
        allowed = (win_alive[None, None, :] > 0) | diagonal[None]
        row_peak = lax.optimization_barrier(jnp.max(jnp.where(allowed, scores, -1e+30), axis=-1, keepdims=True))
        raw = jnp.where(allowed, jnp.exp(scores - row_peak), 0.0)
        weights_bf = (raw / lax.optimization_barrier(jnp.sum(raw, axis=-1, keepdims=True))).astype(jnp.bfloat16)
        return jnp.einsum('hqk,khd->qhd', weights_bf.astype(jnp.float32), win_v.astype(jnp.float32)).astype(jnp.bfloat16)
    attended = lax.map(per_window, (rolled_q, rolled_k, rolled_v, rolled_alive))
    attended = jnp.roll(attended.reshape(TOKENS, D), half_win, axis=0)
    mixing = jnp.dot(attended, out_weight, preferred_element_type=jnp.float32)
    tokens_out = (mixed_in + mixing).T.astype(jnp.bfloat16)
    return (conv_out, tokens_out)
```

```python
import functools

import jax
import jax.numpy as jnp
import numpy as np
from jax import lax
from jax.experimental import pallas as pl
from jax.experimental.pallas import tpu as pltpu
from jax.sharding import PartitionSpec as P

MESH = pl.DeviceIdType.MESH
BF = jnp.bfloat16
F32 = jnp.float32
NEG = -1e30
SLABS = (4, 6, 6)
ROWS = 144 * 16
Q_SCALE = 0.125 * 1.4426950408889634


def slab_tables():
    i, j, k, xh, yh, zh = np.meshgrid(
        np.arange(4), np.arange(6), np.arange(6), np.arange(4), np.arange(2), np.arange(2), indexing="ij"
    )
    x, y, z = (2 * xh + i - 1).ravel(), (4 * yh + j - 1).ravel(), (4 * zh + k - 1).ravel()
    inside = [(c >= 0) & (c < 8) for c in (x, y, z)]
    row = np.arange(ROWS)
    voxel_rows = np.zeros((ROWS, 512), np.float32)
    hit = inside[0] & inside[1] & inside[2]
    voxel_rows[row[hit], (64 * x + 8 * y + z)[hit]] = 1
    ghost_rows = np.zeros((ROWS, 384), np.float32)
    for face in range(6):
        axis, upper = face // 2, face % 2
        coord = (x, y, z)[axis]
        others = [c for a, c in enumerate((x, y, z)) if a != axis]
        ok = [inside[a] for a in range(3) if a != axis]
        hit = (coord == (8 if upper else -1)) & ok[0] & ok[1]
        ghost_rows[row[hit], (64 * face + 8 * others[0] + others[1])[hit]] = 1
    faces = np.zeros((512, 384), np.float32)
    cells = np.arange(64)
    high, low = cells // 8, cells % 8
    sources = [448 + cells, cells, 64 * high + 56 + low, 64 * high + low, 64 * high + 8 * low + 7, 64 * high + 8 * low]
    for face in range(6):
        faces[sources[face], 64 * face + cells] = 1
    xl, yl, zl, xh, yh, zh = [
        a.ravel()
        for a in np.meshgrid(*[np.arange(n) for n in (2, 4, 4, 4, 2, 2)], indexing="ij")
    ]
    x, y, z = 2 * xh + xl, 4 * yh + yl, 4 * zh + zl
    order = np.zeros((512, 512), np.float32)
    order[np.arange(512), 64 * x + 8 * y + z] = 1
    p, q, r = x // 2, y // 2, z // 2
    token = 32 * (p // 2) + 16 * (q // 2) + 8 * (r // 2) + 4 * (p % 2) + 2 * (q % 2) + r % 2
    pool = np.zeros((64, 512), np.float32)
    pool[token, np.arange(512)] = 0.125
    return [jnp.asarray(t, BF) for t in (voxel_rows, ghost_rows, faces, order, pool)]


def dot(a, b):
    return lax.dot_general(a, b, (((1,), (0,)), ((), ())), preferred_element_type=F32)


def dot_nt(a, b):
    return lax.dot_general(a, b, (((1,), (1,)), ((), ())), preferred_element_type=F32)


def kernel(
    n_space,
    n_chan,
    occ_ref,
    nbr_ref,
    bias_ref,
    gain_ref,
    proj_ref,
    feat_hbm,
    conv_w_hbm,
    latent_hbm,
    qkv_hbm,
    out_w_hbm,
    vox_hbm,
    ghost_hbm,
    face_hbm,
    order_hbm,
    pool_hbm,
    conv_out_ref,
    tokens_ref,
    feat,
    conv_w,
    lat,
    qkv_w,
    out_w,
    vox_t,
    ghost_t,
    face_t,
    order_t,
    pool_t,
    store,
    ghosts,
    slabs,
    block_w,
    masked_s,
    conv_s,
    pooled,
    proj_t,
    qw_t,
    vw_t,
    ow_t,
    base_t,
    mask,
    keys,
    vals,
    qry,
    att,
    load_sem,
    send_sem,
    recv_sem,
):
    count = n_space * n_chan
    me = lax.axis_index("space") * n_chan + lax.axis_index("chan")
    core = me % 2
    chip = me // 2

    def place(index):
        index = (index + count) % count
        return (index // n_chan, index % n_chan)

    barrier = pltpu.get_barrier_semaphore()
    for step in (-2, -1, 1, 2):
        pl.semaphore_signal(barrier, inc=1, device_id=place(me + step), device_id_type=MESH)

    loads = {}
    for index, (name, src, dst) in enumerate(
        (
            ("feat", feat_hbm, feat),
            ("face", face_hbm, face_t),
            ("vox", vox_hbm, vox_t),
            ("order", order_hbm, order_t),
            ("conv_w", conv_w_hbm, conv_w),
            ("ghost", ghost_hbm, ghost_t),
            ("lat", latent_hbm, lat.at[pl.ds(512, 1024)]),
            ("qkv", qkv_hbm, qkv_w),
            ("out_w", out_w_hbm, out_w),
            ("pool", pool_hbm, pool_t),
        )
    ):
        loads[name] = pltpu.make_async_copy(src, dst, load_sem.at[index])
        loads[name].start()

    def remote(src, dst, send, recv, target):
        return pltpu.make_async_remote_copy(
            src_ref=src,
            dst_ref=dst,
            send_sem=send_sem.at[send],
            recv_sem=recv_sem.at[recv],
            device_id=place(target),
            device_id_type=MESH,
        )

    loads["feat"].wait()
    for b in range(16):
        rows = pl.ds(b * 32, 32)
        block = feat[rows, :]
        feat[rows, :] = jnp.where(occ_ref[b] > 0, block, jnp.zeros_like(block))
    loads["face"].wait()
    own_faces = dot(feat[...], face_t[...]).astype(BF).reshape(16, 32, 384)
    store[pl.ds(pl.multiple_of(core * 16, 16), 16)] = own_faces
    store[pl.ds(80, 16)] = jnp.zeros((16, 32, 384), BF)

    pl.semaphore_wait(barrier, 4)
    own = store.at[pl.ds(core * 16, 16)]
    shared_slot = 4 - core
    shared_base = 2 * (chip - 1) + 4 * core
    sends = []
    for half in range(2):
        sends.append(
            remote(
                store.at[pl.ds(core * 16 + half * 8, 8)],
                store.at[pl.ds(shared_slot * 16 + half * 8, 8)],
                half,
                1 - core,
                shared_base + half,
            )
        )
    sends.append(remote(own, own, 2, 2, me + 1 - 2 * core))
    sends.append(remote(own, store.at[pl.ds(32, 16)], 3, 3, me + 2 - 4 * core))
    for copy in sends:
        copy.start()

    loads["vox"].wait()
    for g in range(2):
        block = feat[pl.ds(g * 256, 256), :]
        for i in range(4):
            part = dot_nt(vox_t[pl.ds(i * 576, 576), :], block).astype(BF)
            slabs[g, i] = part.reshape(6, 6, 16, 256)
    loads["order"].wait()
    masked_s[...] = dot_nt(feat[...], order_t[...]).astype(BF)

    loads["conv_w"].wait()
    rep_row = lax.broadcasted_iota(jnp.int32, (32, 256), 0)
    rep_lane = lax.broadcasted_iota(jnp.int32, (32, 256), 1)
    spread = (rep_lane % 32 == rep_row).astype(F32).astype(BF)

    def block_tap(tap, carry):
        wide = dot(conv_w[tap], spread).astype(BF)
        for b in range(8):
            block_w[tap, pl.ds(b * 32, 32), :] = jnp.where(rep_lane // 32 == b, wide, jnp.zeros_like(wide))
        return carry

    lax.fori_loop(0, 27, block_tap, 0)

    eye_row = lax.broadcasted_iota(jnp.int32, (512, 512), 0)
    eye_lane = lax.broadcasted_iota(jnp.int32, (512, 512), 1)
    eye = (eye_row == eye_lane).astype(F32).astype(BF)
    loads["qkv"].wait()
    loads["out_w"].wait()
    qw_t[...] = dot_nt(eye, qkv_w[0]).astype(BF)
    vw_t[...] = dot_nt(eye, qkv_w[2]).astype(BF)
    ow_t[...] = dot_nt(eye, out_w[...]).astype(BF)
    proj_tile = jnp.concatenate([proj_ref[...]] * 8, axis=0)
    proj_t[...] = dot_nt(eye, proj_tile).astype(BF)

    small_row = lax.broadcasted_iota(jnp.int32, (32, 32), 0)
    small_lane = lax.broadcasted_iota(jnp.int32, (32, 32), 1)
    bias_col = jnp.sum(jnp.where(small_row == small_lane, bias_ref[...], 0.0), axis=1, keepdims=True)

    m_row = lax.broadcasted_iota(jnp.int32, (64, 512), 0)
    m_lane = lax.broadcasted_iota(jnp.int32, (64, 512), 1)
    for b in range(16):
        half, slot = b // 8, b % 8
        level = jnp.where(occ_ref[b] > 0, 0.0, NEG)
        base = 512 if half == 0 else 0
        mask[half, pl.ds(base + slot * 64, 64), :] = jnp.where(m_row + slot * 64 == m_lane, 0.0, level)

    occ_lane = lax.broadcasted_iota(jnp.int32, (16, 256), 1) // 32
    for g in range(2):
        row = jnp.zeros((16, 256), F32)
        for b in range(8):
            row = jnp.where(occ_lane == b, occ_ref[g * 8 + b].astype(F32), row)
        pooled[1 + g, pl.ds(64, 16), :] = row.astype(BF)

    for h in range(8):
        vals[h, pl.ds(64, 16), :] = jnp.ones((16, 2048), BF)
        qry[h, pl.ds(64 * (1 - h % 2), 64), :] = jnp.zeros((64, 1024), BF)

    loads["ghost"].wait()
    loads["pool"].wait()
    loads["lat"].wait()

    forwards = []
    for index, slot in ((0, 3), (1, 4)):
        part = store.at[pl.ds(slot * 16 + core * 8, 8)]
        remote(part, part, 4 + index, index, me + 1 - 2 * core).wait_recv()
        forward = remote(part, part, 4 + index, 4 + index, me + 1 - 2 * core)
        forward.start()
        forwards.append(forward)
    sends[2].wait_recv()
    sends[3].wait_recv()
    for index, slot in ((0, 3), (1, 4)):
        part = store.at[pl.ds(slot * 16 + (1 - core) * 8, 8)]
        remote(part, part, 4 + index, 4 + index, me + 1 - 2 * core).wait_recv()

    lat_sends = [
        remote(lat.at[pl.ds(512, 512)], lat.at[pl.ds(1536, 512)], 6, 6, me - 1),
        remote(lat.at[pl.ds(1024, 512)], lat.at[pl.ds(0, 512)], 7, 7, me + 1),
    ]
    for copy in lat_sends:
        copy.start()

    half_lane = lax.broadcasted_iota(jnp.int32, (32, 128), 1) < 64

    def pick(b, carry):
        for pair in range(3):
            parts = []
            for side in range(2):
                peer = nbr_ref[b, 2 * pair + side]
                rel = peer // 16 - 2 * chip
                slot = jnp.where(
                    rel == 0, 0, jnp.where(rel == 1, 1, jnp.where(rel == -1, 3, jnp.where(rel == 2, 4, 2)))
                )
                row = jnp.where(peer >= 0, slot * 16 + peer % 16, 80)
                parts.append(store[row, :, pl.ds(pair * 128, 128)])
            ghosts[pl.ds(b * 32, 32), pl.ds(pair * 128, 128)] = jnp.where(half_lane, parts[0], parts[1])
        return carry

    lax.fori_loop(0, 16, pick, 0)

    for g in range(2):
        block = ghosts[pl.ds(g * 256, 256), :]
        for i in range(4):
            part = dot_nt(ghost_t[pl.ds(i * 576, 576), :], block).astype(BF)
            slabs[g, i] = slabs[g, i] + part.reshape(6, 6, 16, 256)

    def conv_group(g, carry):
        total = jnp.zeros((256, 512), F32)
        for tap in range(27):
            i, j, k = tap // 9, tap // 3 % 3, tap % 3
            patch = slabs[g, pl.ds(i, 2), pl.ds(j, 4), pl.ds(k, 4)].reshape(512, 256)
            total = total + dot_nt(block_w[tap], patch)
        rows = pl.ds(pl.multiple_of(g * 256, 256), 256)
        conv_s[rows, :] = total
        return carry

    lax.fori_loop(0, 2, conv_group, 0)
    for g in range(2):
        parts = []
        for b in range(8):
            rows = pl.ds(g * 256 + b * 32, 32)
            pre = conv_s[rows, :] + bias_col
            mixed = masked_s[rows, :].astype(F32) + pre / (1.0 + jnp.exp(-pre))
            parts.append(jnp.where(occ_ref[g * 8 + b] > 0, mixed, 0.0).astype(BF))
        conv_g = jnp.concatenate(parts, axis=0)
        pooled[1 + g, pl.ds(0, 64), :] = dot_nt(pool_t[...], conv_g).astype(BF)
        masked_s[pl.ds(g * 256, 256), :] = conv_g

    pool_sends = [
        remote(pooled.at[1], pooled.at[3], 8, 8, me - 1),
        remote(pooled.at[2], pooled.at[0], 9, 9, me + 1),
    ]
    for copy in pool_sends:
        copy.start()
    conv_out_ref[...] = dot(masked_s[...], order_t[...]).astype(BF)

    wide_row = lax.broadcasted_iota(jnp.int32, (512, 256), 0)
    wide_lane = lax.broadcasted_iota(jnp.int32, (512, 256), 1)
    same_brick = wide_row // 64 == wide_lane // 32
    first_lane = same_brick & (wide_lane % 32 == 0)
    for g in (1, 2, 0, 3):
        if g == 0:
            lat_sends[0].wait_recv()
            lat_sends[1].wait_recv()
            pool_sends[0].wait_recv()
            pool_sends[1].wait_recv()
        cells = pooled[g, pl.ds(0, 64), :]
        tall = jnp.concatenate([cells] * 8, axis=0)
        tall = jnp.where(same_brick, tall, jnp.zeros_like(tall))
        latent = lat[pl.ds(g * 512, 512), :]
        mixed = latent.astype(F32) + dot(tall, proj_tile)
        scale = lax.rsqrt(jnp.mean(mixed * mixed, axis=-1, keepdims=True) + 1e-06)
        normed = (mixed * scale * gain_ref[...]).astype(BF)
        k_all = dot(normed, qkv_w[1]).astype(BF)
        for pair in range(4):
            keys[pair, pl.ds(g * 512, 512), :] = k_all[:, pair * 128 : pair * 128 + 128]
        v_all = dot_nt(vw_t[...], normed).astype(BF)
        for h in range(8):
            vals[h, pl.ds(0, 64), pl.ds(g * 512, 512)] = v_all[h * 64 : h * 64 + 64]
        if g in (1, 2):
            lanes = pl.ds((g - 1) * 512, 512)
            q_all = (dot_nt(qw_t[...], normed) * Q_SCALE).astype(BF)
            for h in range(8):
                qry[h, pl.ds(64 * (h % 2), 64), lanes] = q_all[h * 64 : h * 64 + 64]
            base_t[:, lanes] = dot_nt(eye, latent) + dot_nt(proj_t[...], tall)
        else:
            alive = jnp.broadcast_to(pooled[g, pl.ds(64, 16), :][:1], (128, 256))
            level = dot_nt(first_lane.astype(F32).astype(BF), alive)
            level = jnp.where(level > 0.5, 0.0, NEG)
            half, start = (0, 0) if g == 0 else (1, 512)
            mask[half, pl.ds(start, 512), :] = jnp.concatenate([level] * 4, axis=1)

    for half in range(2):

        def pair_step(pair, carry):
            k_pair = keys[pair, pl.ds(half * 1024, 1024), :]
            for side in range(2):
                h = pair * 2 + side
                scores = dot(k_pair, qry[h, :, pl.ds(half * 512, 512)]) + mask[half]
                peak = jnp.max(scores, axis=0, keepdims=True)
                weights = jnp.exp2(scores - peak).astype(BF)
                out = dot(vals[h, :, pl.ds(half * 1024, 1024)], weights)
                out = (out[:64] / out[64:65]).astype(BF)
                att[pl.ds(pl.multiple_of(h * 64, 64), 64), pl.ds(half * 512, 512)] = out
            return carry

        lax.fori_loop(0, 4, pair_step, 0)
        lanes = pl.ds(half * 512, 512)
        tokens_ref[:, lanes] = (base_t[:, lanes] + dot(ow_t[...], att[:, lanes])).astype(BF)

    for copy in sends + forwards + lat_sends + pool_sends:
        copy.wait_send()


def local(n_space, n_chan, features, occupancy, neighbours, conv_weight, conv_bias, latent, token_proj, norm_gain, qkv_weight, out_weight):
    tables = slab_tables()
    smem = pl.BlockSpec(memory_space=pltpu.SMEM)
    vmem = pl.BlockSpec(memory_space=pltpu.VMEM)
    hbm = pl.BlockSpec(memory_space=pl.ANY)
    conv_out, tokens_out = pl.pallas_call(
        functools.partial(kernel, n_space, n_chan),
        out_shape=(jax.ShapeDtypeStruct((512, 512), BF), jax.ShapeDtypeStruct((512, 1024), BF)),
        in_specs=[smem, smem, vmem, vmem, vmem] + [hbm] * 10,
        out_specs=(vmem, vmem),
        scratch_shapes=[
            pltpu.VMEM((512, 512), BF),
            pltpu.VMEM((27, 32, 32), BF),
            pltpu.VMEM((2048, 512), BF),
            pltpu.VMEM((3, 512, 512), BF),
            pltpu.VMEM((512, 512), BF),
            pltpu.VMEM((ROWS, 512), BF),
            pltpu.VMEM((ROWS, 384), BF),
            pltpu.VMEM((512, 384), BF),
            pltpu.VMEM((512, 512), BF),
            pltpu.VMEM((64, 512), BF),
            pltpu.VMEM((96, 32, 384), BF),
            pltpu.VMEM((512, 384), BF),
            pltpu.VMEM((2,) + SLABS + (16, 256), BF),
            pltpu.VMEM((27, 256, 256), BF),
            pltpu.VMEM((512, 512), BF),
            pltpu.VMEM((512, 512), F32),
            pltpu.VMEM((4, 80, 256), BF),
            pltpu.VMEM((512, 256), BF),
            pltpu.VMEM((512, 512), BF),
            pltpu.VMEM((512, 512), BF),
            pltpu.VMEM((512, 512), BF),
            pltpu.VMEM((512, 1024), F32),
            pltpu.VMEM((2, 1024, 512), F32),
            pltpu.VMEM((4, 2048, 128), BF),
            pltpu.VMEM((8, 80, 2048), BF),
            pltpu.VMEM((8, 128, 1024), BF),
            pltpu.VMEM((512, 1024), BF),
            pltpu.SemaphoreType.DMA((10,)),
            pltpu.SemaphoreType.DMA((10,)),
            pltpu.SemaphoreType.DMA((10,)),
        ],
        compiler_params=pltpu.CompilerParams(
            collective_id=0, has_side_effects=True, vmem_limit_bytes=60 * 1024 * 1024
        ),
        cost_estimate=pl.CostEstimate(flops=8 * 10**9, bytes_accessed=12 * 10**6, transcendentals=9 * 10**6),
    )(
        occupancy,
        neighbours,
        conv_bias.reshape(1, 32),
        norm_gain.reshape(1, 512),
        token_proj,
        features.reshape(512, 512),
        conv_weight,
        latent,
        qkv_weight,
        out_weight,
        *tables,
    )
    return conv_out.reshape(16, 32, 512), tokens_out


def solution(mesh):
    both = ("space", "chan")
    return jax.shard_map(
        functools.partial(local, mesh.shape["space"], mesh.shape["chan"]),
        mesh=mesh,
        in_specs=(
            P(both, None, None),
            P(both),
            P(both, None),
            P(),
            P(),
            P(both, None),
            P(),
            P(),
            P(),
            P(),
        ),
        out_specs=(P(both, None, None), P(None, both)),
        check_vma=False,
    )
```

```python
import functools

import jax
import jax.numpy as jnp
import numpy as np
from jax import lax
from jax.experimental import pallas as pl
from jax.experimental.pallas import tpu as pltpu
from jax.sharding import PartitionSpec as P

MESH = pl.DeviceIdType.MESH
BF = jnp.bfloat16
F32 = jnp.float32
NEG = -1e30
SLABS = (4, 6, 6)
ROWS = 144 * 16
Q_SCALE = 0.125 * 1.4426950408889634


def slab_tables():
    i, j, k, xh, yh, zh = np.meshgrid(
        np.arange(4), np.arange(6), np.arange(6), np.arange(4), np.arange(2), np.arange(2), indexing="ij"
    )
    x, y, z = (2 * xh + i - 1).ravel(), (4 * yh + j - 1).ravel(), (4 * zh + k - 1).ravel()
    inside = [(c >= 0) & (c < 8) for c in (x, y, z)]
    row = np.arange(ROWS)
    voxel_rows = np.zeros((ROWS, 512), np.float32)
    hit = inside[0] & inside[1] & inside[2]
    voxel_rows[row[hit], (64 * x + 8 * y + z)[hit]] = 1
    ghost_rows = np.zeros((ROWS, 384), np.float32)
    for face in range(6):
        axis, upper = face // 2, face % 2
        coord = (x, y, z)[axis]
        others = [c for a, c in enumerate((x, y, z)) if a != axis]
        ok = [inside[a] for a in range(3) if a != axis]
        hit = (coord == (8 if upper else -1)) & ok[0] & ok[1]
        ghost_rows[row[hit], (64 * face + 8 * others[0] + others[1])[hit]] = 1
    faces = np.zeros((512, 384), np.float32)
    cells = np.arange(64)
    high, low = cells // 8, cells % 8
    sources = [448 + cells, cells, 64 * high + 56 + low, 64 * high + low, 64 * high + 8 * low + 7, 64 * high + 8 * low]
    for face in range(6):
        faces[sources[face], 64 * face + cells] = 1
    xl, yl, zl, xh, yh, zh = [
        a.ravel()
        for a in np.meshgrid(*[np.arange(n) for n in (2, 4, 4, 4, 2, 2)], indexing="ij")
    ]
    x, y, z = 2 * xh + xl, 4 * yh + yl, 4 * zh + zl
    order = np.zeros((512, 512), np.float32)
    order[np.arange(512), 64 * x + 8 * y + z] = 1
    p, q, r = x // 2, y // 2, z // 2
    token = 32 * (p // 2) + 16 * (q // 2) + 8 * (r // 2) + 4 * (p % 2) + 2 * (q % 2) + r % 2
    pool = np.zeros((64, 512), np.float32)
    pool[token, np.arange(512)] = 0.125
    return [jnp.asarray(t, BF) for t in (voxel_rows, ghost_rows, faces, order, pool)]


def dot(a, b):
    return lax.dot_general(a, b, (((1,), (0,)), ((), ())), preferred_element_type=F32)


def dot_nt(a, b):
    return lax.dot_general(a, b, (((1,), (1,)), ((), ())), preferred_element_type=F32)


def kernel(
    n_space,
    n_chan,
    occ_ref,
    nbr_ref,
    bias_ref,
    gain_ref,
    proj_ref,
    feat_hbm,
    conv_w_hbm,
    latent_hbm,
    qkv_hbm,
    out_w_hbm,
    vox_hbm,
    ghost_hbm,
    face_hbm,
    order_hbm,
    pool_hbm,
    conv_out_ref,
    tokens_ref,
    feat,
    conv_w,
    lat,
    qkv_w,
    out_w,
    vox_t,
    ghost_t,
    face_t,
    order_t,
    pool_t,
    store,
    ghosts,
    slabs,
    block_w,
    masked_s,
    conv_s,
    pooled,
    proj_t,
    qw_t,
    vw_t,
    ow_t,
    base_t,
    mask,
    keys,
    vals,
    qry,
    att,
    even_s,
    odd_s,
    parts_s,
    load_sem,
    send_sem,
    recv_sem,
):
    count = n_space * n_chan
    me = lax.axis_index("space") * n_chan + lax.axis_index("chan")
    core = me % 2
    chip = me // 2

    def place(index):
        index = (index + count) % count
        return (index // n_chan, index % n_chan)

    barrier = pltpu.get_barrier_semaphore()
    for step in (-2, -1, 1, 2):
        pl.semaphore_signal(barrier, inc=1, device_id=place(me + step), device_id_type=MESH)

    loads = {}
    for index, (name, src, dst) in enumerate(
        (
            ("feat", feat_hbm, feat),
            ("face", face_hbm, face_t),
            ("vox", vox_hbm, vox_t),
            ("order", order_hbm, order_t),
            ("conv_w", conv_w_hbm, conv_w),
            ("ghost", ghost_hbm, ghost_t),
            ("lat", latent_hbm, lat.at[pl.ds(512, 1024)]),
            ("qkv", qkv_hbm, qkv_w),
            ("out_w", out_w_hbm, out_w),
            ("pool", pool_hbm, pool_t),
        )
    ):
        loads[name] = pltpu.make_async_copy(src, dst, load_sem.at[index])
        loads[name].start()

    def remote(src, dst, send, recv, target):
        return pltpu.make_async_remote_copy(
            src_ref=src,
            dst_ref=dst,
            send_sem=send_sem.at[send],
            recv_sem=recv_sem.at[recv],
            device_id=place(target),
            device_id_type=MESH,
        )

    loads["feat"].wait()
    for b in range(16):
        rows = pl.ds(b * 32, 32)
        block = feat[rows, :]
        feat[rows, :] = jnp.where(occ_ref[b] > 0, block, jnp.zeros_like(block))
    loads["face"].wait()
    own_faces = dot(feat[...], face_t[...]).astype(BF).reshape(16, 32, 384)
    store[pl.ds(pl.multiple_of(core * 16, 16), 16)] = own_faces
    store[pl.ds(80, 16)] = jnp.zeros((16, 32, 384), BF)

    pl.semaphore_wait(barrier, 4)
    own = store.at[pl.ds(core * 16, 16)]
    shared_slot = 4 - core
    shared_base = 2 * (chip - 1) + 4 * core
    sends = []
    for half in range(2):
        sends.append(
            remote(
                store.at[pl.ds(core * 16 + half * 8, 8)],
                store.at[pl.ds(shared_slot * 16 + half * 8, 8)],
                half,
                1 - core,
                shared_base + half,
            )
        )
    sends.append(remote(own, own, 2, 2, me + 1 - 2 * core))
    sends.append(remote(own, store.at[pl.ds(32, 16)], 3, 3, me + 2 - 4 * core))
    for copy in sends:
        copy.start()

    loads["vox"].wait()
    for g in range(2):
        block = feat[pl.ds(g * 256, 256), :]
        for i in range(4):
            part = dot_nt(vox_t[pl.ds(i * 576, 576), :], block).astype(BF)
            slabs[g, i] = part.reshape(6, 6, 16, 256)
    loads["order"].wait()
    masked_s[...] = dot_nt(feat[...], order_t[...]).astype(BF)

    loads["conv_w"].wait()
    rep_row = lax.broadcasted_iota(jnp.int32, (32, 256), 0)
    rep_lane = lax.broadcasted_iota(jnp.int32, (32, 256), 1)
    spread = (rep_lane % 32 == rep_row).astype(F32).astype(BF)

    def block_tap(tap, carry):
        wide = dot(conv_w[tap], spread).astype(BF)
        for b in range(8):
            block_w[tap, pl.ds(b * 32, 32), :] = jnp.where(rep_lane // 32 == b, wide, jnp.zeros_like(wide))
        return carry

    lax.fori_loop(0, 27, block_tap, 0)

    eye_row = lax.broadcasted_iota(jnp.int32, (512, 512), 0)
    eye_lane = lax.broadcasted_iota(jnp.int32, (512, 512), 1)
    eye = (eye_row == eye_lane).astype(F32).astype(BF)
    loads["qkv"].wait()
    loads["out_w"].wait()
    qw_t[...] = dot_nt(eye, qkv_w[0]).astype(BF)
    vw_t[...] = dot_nt(eye, qkv_w[2]).astype(BF)
    ow_t[...] = dot_nt(eye, out_w[...]).astype(BF)
    proj_tile = jnp.concatenate([proj_ref[...]] * 8, axis=0)
    proj_t[...] = dot_nt(eye, proj_tile).astype(BF)

    small_row = lax.broadcasted_iota(jnp.int32, (32, 32), 0)
    small_lane = lax.broadcasted_iota(jnp.int32, (32, 32), 1)
    bias_col = jnp.sum(jnp.where(small_row == small_lane, bias_ref[...], 0.0), axis=1, keepdims=True)

    m_row = lax.broadcasted_iota(jnp.int32, (64, 512), 0)
    m_lane = lax.broadcasted_iota(jnp.int32, (64, 512), 1)
    for b in range(16):
        half, slot = b // 8, b % 8
        level = jnp.where(occ_ref[b] > 0, 0.0, NEG)
        mask[0, half, pl.ds(slot * 64, 64), :] = jnp.where(m_row + slot * 64 == m_lane, 0.0, level)

    occ_lane = lax.broadcasted_iota(jnp.int32, (16, 256), 1) // 32
    for g in range(2):
        row = jnp.zeros((16, 256), F32)
        for b in range(8):
            row = jnp.where(occ_lane == b, occ_ref[g * 8 + b].astype(F32), row)
        pooled[1 + g, pl.ds(64, 16), :] = row.astype(BF)

    for h in range(8):
        vals[h, pl.ds(64, 16), :] = jnp.ones((16, 2048), BF)
        qry[h, pl.ds(64 * (1 - h % 2), 64), :] = jnp.zeros((64, 1024), BF)

    loads["ghost"].wait()
    loads["pool"].wait()
    loads["lat"].wait()

    forwards = []
    for index, slot in ((0, 3), (1, 4)):
        part = store.at[pl.ds(slot * 16 + core * 8, 8)]
        remote(part, part, 4 + index, index, me + 1 - 2 * core).wait_recv()
        forward = remote(part, part, 4 + index, 4 + index, me + 1 - 2 * core)
        forward.start()
        forwards.append(forward)
    sends[2].wait_recv()
    sends[3].wait_recv()
    for index, slot in ((0, 3), (1, 4)):
        part = store.at[pl.ds(slot * 16 + (1 - core) * 8, 8)]
        remote(part, part, 4 + index, 4 + index, me + 1 - 2 * core).wait_recv()

    lat_sends = [
        remote(lat.at[pl.ds(512, 512)], lat.at[pl.ds(1536, 512)], 6, 6, me - 1),
        remote(lat.at[pl.ds(1024, 512)], lat.at[pl.ds(0, 512)], 7, 7, me + 1),
    ]
    for copy in lat_sends:
        copy.start()

    half_lane = lax.broadcasted_iota(jnp.int32, (32, 128), 1) < 64

    def pick(b, carry):
        for pair in range(3):
            parts = []
            for side in range(2):
                peer = nbr_ref[2 * pair + side, b]
                rel = peer // 16 - 2 * chip
                slot = jnp.where(
                    rel == 0, 0, jnp.where(rel == 1, 1, jnp.where(rel == -1, 3, jnp.where(rel == 2, 4, 2)))
                )
                row = jnp.where(peer >= 0, slot * 16 + peer % 16, 80)
                parts.append(store[row, :, pl.ds(pair * 128, 128)])
            ghosts[pl.ds(b * 32, 32), pl.ds(pair * 128, 128)] = jnp.where(half_lane, parts[0], parts[1])
        return carry

    lax.fori_loop(0, 16, pick, 0)

    for g in range(2):
        block = ghosts[pl.ds(g * 256, 256), :]
        for i in range(4):
            part = dot_nt(ghost_t[pl.ds(i * 576, 576), :], block).astype(BF)
            slabs[g, i] = slabs[g, i] + part.reshape(6, 6, 16, 256)

    def conv_group(g, carry):
        total = jnp.zeros((256, 512), F32)
        for tap in range(27):
            i, j, k = tap // 9, tap // 3 % 3, tap % 3
            patch = slabs[g, pl.ds(i, 2), pl.ds(j, 4), pl.ds(k, 4)].reshape(512, 256)
            total = total + dot_nt(block_w[tap], patch)
        rows = pl.ds(pl.multiple_of(g * 256, 256), 256)
        conv_s[rows, :] = total
        return carry

    lax.fori_loop(0, 2, conv_group, 0)
    for g in range(2):
        parts = []
        for b in range(8):
            rows = pl.ds(g * 256 + b * 32, 32)
            pre = conv_s[rows, :] + bias_col
            mixed = masked_s[rows, :].astype(F32) + pre / (1.0 + jnp.exp(-pre))
            parts.append(jnp.where(occ_ref[g * 8 + b] > 0, mixed, 0.0).astype(BF))
        conv_g = jnp.concatenate(parts, axis=0)
        pooled[1 + g, pl.ds(0, 64), :] = dot_nt(pool_t[...], conv_g).astype(BF)
        masked_s[pl.ds(g * 256, 256), :] = conv_g

    pool_sends = [
        remote(pooled.at[1], pooled.at[3], 8, 8, me - 1),
        remote(pooled.at[2], pooled.at[0], 9, 9, me + 1),
    ]
    for copy in pool_sends:
        copy.start()
    conv_out_ref[...] = dot(masked_s[...], order_t[...]).astype(BF)

    wide_row = lax.broadcasted_iota(jnp.int32, (512, 256), 0)
    wide_lane = lax.broadcasted_iota(jnp.int32, (512, 256), 1)
    same_brick = wide_row // 64 == wide_lane // 32
    first_lane = same_brick & (wide_lane % 32 == 0)
    def project(g):
        cells = pooled[g, pl.ds(0, 64), :]
        tall = jnp.concatenate([cells] * 8, axis=0)
        tall = jnp.where(same_brick, tall, jnp.zeros_like(tall))
        latent = lat[pl.ds(g * 512, 512), :]
        mixed = latent.astype(F32) + dot(tall, proj_tile)
        scale = lax.rsqrt(jnp.mean(mixed * mixed, axis=-1, keepdims=True) + 1e-06)
        normed = (mixed * scale * gain_ref[...]).astype(BF)
        k_all = dot(normed, qkv_w[1]).astype(BF)
        for pair in range(4):
            keys[pair, pl.ds(g * 512, 512), :] = k_all[:, pair * 128 : pair * 128 + 128]
        v_all = dot_nt(vw_t[...], normed).astype(BF)
        for h in range(8):
            vals[h, pl.ds(0, 64), pl.ds(g * 512, 512)] = v_all[h * 64 : h * 64 + 64]
        if g in (1, 2):
            lanes = pl.ds((g - 1) * 512, 512)
            q_all = (dot_nt(qw_t[...], normed) * Q_SCALE).astype(BF)
            for h in range(8):
                qry[h, pl.ds(64 * (h % 2), 64), lanes] = q_all[h * 64 : h * 64 + 64]
            base_t[:, lanes] = dot_nt(eye, latent) + dot_nt(proj_t[...], tall)
        else:
            alive = jnp.broadcast_to(pooled[g, pl.ds(64, 16), :][:1], (128, 256))
            level = dot_nt(first_lane.astype(F32).astype(BF), alive)
            level = jnp.where(level > 0.5, 0.0, NEG)
            mask[1, g // 3] = jnp.concatenate([level] * 4, axis=1)

    def score_chunk(side, half, pair, h, chunk, dst):
        rows = pl.ds(chunk * 256, 256)
        base = 512 + half * 512 if side == 0 else half * 1536
        part = dot(keys[pair, pl.ds(base + chunk * 256, 256), :], qry[h, :, pl.ds(half * 512, 512)])
        part = part + mask[side, half, rows, :]
        dst[rows, :] = part
        return jnp.max(part.reshape(32, 8, 512), axis=0)

    def head_step(side, half, h, now, peaks, nxt, n_half, n_pair, n_head):
        lanes = pl.ds(half * 512, 512)
        base = 512 + half * 512 if side == 0 else half * 1536
        peak = jnp.max(peaks, axis=0, keepdims=True)
        if side == 1:
            own_peak = parts_s[h, pl.ds(72, 8), lanes][:1]
            peak = jnp.maximum(peak, own_peak)
        new_peaks, total = None, None
        for chunk in range(2):
            if nxt is not None:
                top = score_chunk(side, n_half, n_pair, n_head, chunk, nxt)
                new_peaks = top if chunk == 0 else jnp.maximum(new_peaks, top)
            weights = jnp.exp2(now[pl.ds(chunk * 256, 256), :] - peak).astype(BF)
            part = dot(vals[h, :, pl.ds(base + chunk * 256, 256)], weights)
            total = part if chunk == 0 else total + part
        if side == 0:
            parts_s[h, pl.ds(0, 72), lanes] = total[:72]
            parts_s[h, pl.ds(72, 8), lanes] = jnp.broadcast_to(peak, (8, 512))
        else:
            total = total[:72] + parts_s[h, pl.ds(0, 72), lanes] * jnp.exp2(own_peak - peak)
            out = (total[:64] / total[64:65]).astype(BF)
            att[pl.ds(pl.multiple_of(h * 64, 64), 64), lanes] = out
        return new_peaks

    def attend(side):
        peaks = None
        for chunk in range(2):
            top = score_chunk(side, 0, 0, 0, chunk, even_s)
            peaks = top if chunk == 0 else jnp.maximum(peaks, top)
        for half in range(2):

            def pair_step(pair, tops):
                tops = head_step(side, half, pair * 2, even_s, tops, odd_s, half, pair, pair * 2 + 1)
                return head_step(side, half, pair * 2 + 1, odd_s, tops, even_s, half, pair + 1, pair * 2 + 2)

            peaks = lax.fori_loop(0, 3, pair_step, peaks)
            peaks = head_step(side, half, 6, even_s, peaks, odd_s, half, 3, 7)
            peaks = head_step(side, half, 7, odd_s, peaks, even_s if half == 0 else None, 1, 0, 0)
            if side == 1:
                lanes = pl.ds(half * 512, 512)
                tokens_ref[:, lanes] = (base_t[:, lanes] + dot(ow_t[...], att[:, lanes])).astype(BF)

    project(1)
    project(2)
    attend(0)
    for copy in lat_sends + pool_sends:
        copy.wait_recv()
    project(0)
    project(3)
    attend(1)

    for copy in sends + forwards + lat_sends + pool_sends:
        copy.wait_send()


def local(n_space, n_chan, features, occupancy, neighbours, conv_weight, conv_bias, latent, token_proj, norm_gain, qkv_weight, out_weight):
    tables = slab_tables()
    smem = pl.BlockSpec(memory_space=pltpu.SMEM)
    vmem = pl.BlockSpec(memory_space=pltpu.VMEM)
    hbm = pl.BlockSpec(memory_space=pl.ANY)
    conv_out, tokens_out = pl.pallas_call(
        functools.partial(kernel, n_space, n_chan),
        out_shape=(pltpu.VMEM((512, 512), BF), pltpu.VMEM((512, 1024), BF)),
        in_specs=[smem, smem, vmem, vmem, vmem] + [hbm] * 10,
        out_specs=(vmem, vmem),
        scratch_shapes=[
            pltpu.VMEM((512, 512), BF),
            pltpu.VMEM((27, 32, 32), BF),
            pltpu.VMEM((2048, 512), BF),
            pltpu.VMEM((3, 512, 512), BF),
            pltpu.VMEM((512, 512), BF),
            pltpu.VMEM((ROWS, 512), BF),
            pltpu.VMEM((ROWS, 384), BF),
            pltpu.VMEM((512, 384), BF),
            pltpu.VMEM((512, 512), BF),
            pltpu.VMEM((64, 512), BF),
            pltpu.VMEM((96, 32, 384), BF),
            pltpu.VMEM((512, 384), BF),
            pltpu.VMEM((2,) + SLABS + (16, 256), BF),
            pltpu.VMEM((27, 256, 256), BF),
            pltpu.VMEM((512, 512), BF),
            pltpu.VMEM((512, 512), F32),
            pltpu.VMEM((4, 80, 256), BF),
            pltpu.VMEM((512, 256), BF),
            pltpu.VMEM((512, 512), BF),
            pltpu.VMEM((512, 512), BF),
            pltpu.VMEM((512, 512), BF),
            pltpu.VMEM((512, 1024), F32),
            pltpu.VMEM((2, 2, 512, 512), F32),
            pltpu.VMEM((4, 2048, 128), BF),
            pltpu.VMEM((8, 80, 2048), BF),
            pltpu.VMEM((8, 128, 1024), BF),
            pltpu.VMEM((512, 1024), BF),
            pltpu.VMEM((512, 512), F32),
            pltpu.VMEM((512, 512), F32),
            pltpu.VMEM((8, 80, 1024), F32),
            pltpu.SemaphoreType.DMA((10,)),
            pltpu.SemaphoreType.DMA((10,)),
            pltpu.SemaphoreType.DMA((10,)),
        ],
        compiler_params=pltpu.CompilerParams(
            collective_id=0, has_side_effects=True, vmem_limit_bytes=60 * 1024 * 1024
        ),
        cost_estimate=pl.CostEstimate(flops=8 * 10**9, bytes_accessed=12 * 10**6, transcendentals=9 * 10**6),
    )(
        occupancy,
        neighbours.T,
        conv_bias.reshape(1, 32),
        norm_gain.reshape(1, 512),
        token_proj,
        features.reshape(512, 512),
        conv_weight,
        latent,
        qkv_weight,
        out_weight,
        *tables,
    )
    return conv_out.reshape(16, 32, 512), tokens_out


def solution(mesh):
    both = ("space", "chan")
    return jax.shard_map(
        functools.partial(local, mesh.shape["space"], mesh.shape["chan"]),
        mesh=mesh,
        in_specs=(
            P(both, None, None),
            P(both),
            P(both, None),
            P(),
            P(),
            P(both, None),
            P(),
            P(),
            P(),
            P(),
        ),
        out_specs=(P(both, None, None), P(None, both)),
        check_vma=False,
    )
```

```python
import functools

import jax
import jax.numpy as jnp
import numpy as np
from jax import lax
from jax.experimental import pallas as pl
from jax.experimental.pallas import tpu as pltpu
from jax.sharding import PartitionSpec as P

MESH = pl.DeviceIdType.MESH
BF = jnp.bfloat16
F32 = jnp.float32
NEG = -1e30
SLABS = (4, 6, 6)
ROWS = 144 * 16
GHOST_ROWS = 1792
UNITS = 38
HALF = 19
Q_SCALE = 0.125 * 1.4426950408889634


def shell_lane(x, y, z):
    if x in (0, 7):
        return (0 if x == 7 else 64) + 8 * y + z, False
    if y in (0, 7):
        return 128 + (0 if y == 7 else 48) + 8 * (x - 1) + z, False
    index = 6 * (x - 1) + y - 1
    if index < 16:
        return 128 + (96 if z == 7 else 112) + index, False
    return (0 if z == 7 else 20) + index - 16, True


def slab_tables():
    i, j, k, xh, yh, zh = np.meshgrid(
        np.arange(4), np.arange(6), np.arange(6), np.arange(4), np.arange(2), np.arange(2), indexing="ij"
    )
    x, y, z = (2 * xh + i - 1).ravel(), (4 * yh + j - 1).ravel(), (4 * zh + k - 1).ravel()
    inside = [(c >= 0) & (c < 8) for c in (x, y, z)]
    row = np.arange(ROWS)
    voxel_rows = np.zeros((ROWS, 512), np.float32)
    hit = inside[0] & inside[1] & inside[2]
    voxel_rows[row[hit], (64 * x + 8 * y + z)[hit]] = 1
    ghost_rows = np.zeros((ROWS, 768), np.float32)
    for r in range(ROWS):
        cell = (int(x[r]), int(y[r]), int(z[r]))
        out = [a for a in range(3) if not inside[a][r]]
        if len(out) != 1:
            continue
        axis = out[0]
        source = tuple((c % 8) if a == axis else c for a, c in enumerate(cell))
        lane, extra = shell_lane(*source)
        if extra:
            ghost_rows[r, [640 + 40 * third + lane for third in range(3)]] = 1
        else:
            ghost_rows[r, (256, 0, 384)[axis] + lane] = 1
    by_slab = ghost_rows.reshape(4, 6, 6, 16, 768)
    parts = [by_slab[i, 1:5, 1:5] for i in (0, 3)] + [by_slab[:, j] for j in (0, 5)] + [by_slab[:, 1:5, k] for k in (0, 5)]
    ghost_rows = np.concatenate([part.reshape(-1, 768) for part in parts])
    faces = np.zeros((512, 256), np.float32)
    extras = np.zeros((3, 512, 128), np.float32)
    for vx, vy, vz in np.ndindex(8, 8, 8):
        if min(vx, vy, vz) > 0 and max(vx, vy, vz) < 7:
            continue
        lane, extra = shell_lane(vx, vy, vz)
        voxel = 64 * vx + 8 * vy + vz
        if extra:
            for third in range(3):
                extras[third, voxel, 40 * third + lane] = 1
        else:
            faces[voxel, lane] = 1
    xl, yl, zl, xh, yh, zh = [
        a.ravel()
        for a in np.meshgrid(*[np.arange(n) for n in (2, 4, 4, 4, 2, 2)], indexing="ij")
    ]
    x, y, z = 2 * xh + xl, 4 * yh + yl, 4 * zh + zl
    order = np.zeros((512, 512), np.float32)
    order[np.arange(512), 64 * x + 8 * y + z] = 1
    p, q, r = x // 2, y // 2, z // 2
    token = 32 * (p // 2) + 16 * (q // 2) + 8 * (r // 2) + 4 * (p % 2) + 2 * (q % 2) + r % 2
    pool = np.zeros((64, 512), np.float32)
    pool[token, np.arange(512)] = 0.125
    return [jnp.asarray(t, BF) for t in (voxel_rows, ghost_rows, faces, extras, order, pool)]


def dot(a, b):
    return lax.dot_general(a, b, (((1,), (0,)), ((), ())), preferred_element_type=F32)


def dot_nt(a, b):
    return lax.dot_general(a, b, (((1,), (1,)), ((), ())), preferred_element_type=F32)


def kernel(
    n_space,
    n_chan,
    occ_ref,
    nbr_ref,
    bias_ref,
    gain_ref,
    proj_ref,
    feat_hbm,
    conv_w_hbm,
    latent_hbm,
    qkv_hbm,
    out_w_hbm,
    vox_hbm,
    ghost_hbm,
    face_hbm,
    extra_hbm,
    order_hbm,
    pool_hbm,
    conv_out_ref,
    tokens_ref,
    feat,
    conv_w,
    lat,
    qkv_w,
    out_w,
    vox_t,
    ghost_t,
    face_t,
    extra_t,
    order_t,
    pool_t,
    store,
    ghosts,
    slabs,
    block_w,
    masked_s,
    conv_s,
    pooled,
    proj_t,
    qw_t,
    vw_t,
    ow_t,
    base_t,
    mask,
    keys,
    vals,
    qry,
    att,
    even_s,
    odd_s,
    parts_s,
    load_sem,
    send_sem,
    recv_sem,
):
    count = n_space * n_chan
    me = lax.axis_index("space") * n_chan + lax.axis_index("chan")
    core = me % 2
    chip = me // 2

    def place(index):
        index = (index + count) % count
        return (index // n_chan, index % n_chan)

    barrier = pltpu.get_barrier_semaphore()
    for step in (-2, -1, 1, 2):
        pl.semaphore_signal(barrier, inc=1, device_id=place(me + step), device_id_type=MESH)

    loads = {}
    for index, (name, src, dst) in enumerate(
        (
            ("feat", feat_hbm, feat),
            ("face", face_hbm, face_t),
            ("extra", extra_hbm, extra_t),
            ("vox", vox_hbm, vox_t),
            ("order", order_hbm, order_t),
            ("conv_w", conv_w_hbm, conv_w),
            ("ghost", ghost_hbm, ghost_t),
            ("lat", latent_hbm, lat.at[pl.ds(512, 1024)]),
            ("qkv", qkv_hbm, qkv_w),
            ("out_w", out_w_hbm, out_w),
            ("pool", pool_hbm, pool_t),
        )
    ):
        loads[name] = pltpu.make_async_copy(src, dst, load_sem.at[index])
        loads[name].start()

    def remote(src, dst, send, recv, target):
        return pltpu.make_async_remote_copy(
            src_ref=src,
            dst_ref=dst,
            send_sem=send_sem.at[send],
            recv_sem=recv_sem.at[recv],
            device_id=place(target),
            device_id_type=MESH,
        )

    loads["feat"].wait()
    for b in range(16):
        rows = pl.ds(b * 32, 32)
        block = feat[rows, :]
        feat[rows, :] = jnp.where(occ_ref[b] > 0, block, jnp.zeros_like(block))
    loads["face"].wait()
    own_start = core * UNITS
    for tile in range(2):
        cells = dot(feat[...], face_t[:, pl.ds(tile * 128, 128)]).astype(BF)
        store[pl.ds(own_start + tile * 16, 16)] = cells.reshape(16, 32, 128)
    loads["extra"].wait()
    packed = [dot(feat[pl.ds(192 * t, 192 if t < 2 else 128), :], extra_t[t]) for t in range(3)]
    packed = packed[0] + packed[1] + jnp.concatenate([packed[2], jnp.zeros((64, 128), F32)], axis=0)
    store[pl.ds(own_start + 32, 6)] = packed.astype(BF).reshape(6, 32, 128)
    store[pl.ds(5 * UNITS, UNITS)] = jnp.zeros((UNITS, 32, 128), BF)

    pl.semaphore_wait(barrier, 4)
    own = store.at[pl.ds(own_start, UNITS)]
    shared_slot = 4 - core
    shared_base = 2 * (chip - 1) + 4 * core
    sends = []
    for half in range(2):
        sends.append(
            remote(
                store.at[pl.ds(own_start + half * HALF, HALF)],
                store.at[pl.ds(shared_slot * UNITS + half * HALF, HALF)],
                half,
                1 - core,
                shared_base + half,
            )
        )
    sends.append(remote(own, own, 2, 2, me + 1 - 2 * core))
    sends.append(remote(own, store.at[pl.ds(2 * UNITS, UNITS)], 3, 3, me + 2 - 4 * core))
    for copy in sends:
        copy.start()

    loads["vox"].wait()
    for g in range(2):
        block = feat[pl.ds(g * 256, 256), :]
        for i in range(4):
            part = dot_nt(vox_t[pl.ds(i * 576, 576), :], block).astype(BF)
            slabs[g, i] = part.reshape(6, 6, 16, 256)
    loads["order"].wait()
    masked_s[...] = dot_nt(feat[...], order_t[...]).astype(BF)

    loads["conv_w"].wait()
    rep_row = lax.broadcasted_iota(jnp.int32, (32, 256), 0)
    rep_lane = lax.broadcasted_iota(jnp.int32, (32, 256), 1)
    spread = (rep_lane % 32 == rep_row).astype(F32).astype(BF)

    def block_tap(tap, carry):
        wide = dot(conv_w[tap], spread).astype(BF)
        for b in range(8):
            block_w[tap, pl.ds(b * 32, 32), :] = jnp.where(rep_lane // 32 == b, wide, jnp.zeros_like(wide))
        return carry

    lax.fori_loop(0, 27, block_tap, 0)

    eye_row = lax.broadcasted_iota(jnp.int32, (512, 512), 0)
    eye_lane = lax.broadcasted_iota(jnp.int32, (512, 512), 1)
    eye = (eye_row == eye_lane).astype(F32).astype(BF)
    loads["qkv"].wait()
    loads["out_w"].wait()
    qw_t[...] = dot_nt(eye, qkv_w[0]).astype(BF)
    vw_t[...] = dot_nt(eye, qkv_w[2]).astype(BF)
    ow_t[...] = dot_nt(eye, out_w[...]).astype(BF)
    proj_tile = jnp.concatenate([proj_ref[...]] * 8, axis=0)
    proj_t[...] = dot_nt(eye, proj_tile).astype(BF)

    small_row = lax.broadcasted_iota(jnp.int32, (32, 32), 0)
    small_lane = lax.broadcasted_iota(jnp.int32, (32, 32), 1)
    bias_col = jnp.sum(jnp.where(small_row == small_lane, bias_ref[...], 0.0), axis=1, keepdims=True)

    m_row = lax.broadcasted_iota(jnp.int32, (64, 512), 0)
    m_lane = lax.broadcasted_iota(jnp.int32, (64, 512), 1)
    for b in range(16):
        half, slot = b // 8, b % 8
        level = jnp.where(occ_ref[b] > 0, 0.0, NEG)
        mask[0, half, pl.ds(slot * 64, 64), :] = jnp.where(m_row + slot * 64 == m_lane, 0.0, level)

    occ_lane = lax.broadcasted_iota(jnp.int32, (16, 256), 1) // 32
    for g in range(2):
        row = jnp.zeros((16, 256), F32)
        for b in range(8):
            row = jnp.where(occ_lane == b, occ_ref[g * 8 + b].astype(F32), row)
        pooled[1 + g, pl.ds(64, 16), :] = row.astype(BF)

    for h in range(8):
        vals[h, pl.ds(64, 16), :] = jnp.ones((16, 2048), BF)
        qry[h, pl.ds(64 * (1 - h % 2), 64), :] = jnp.zeros((64, 1024), BF)

    loads["ghost"].wait()
    loads["pool"].wait()
    loads["lat"].wait()

    forwards = []
    for index, slot in ((0, 3), (1, 4)):
        part = store.at[pl.ds(slot * UNITS + core * HALF, HALF)]
        remote(part, part, 4 + index, index, me + 1 - 2 * core).wait_recv()
        forward = remote(part, part, 4 + index, 4 + index, me + 1 - 2 * core)
        forward.start()
        forwards.append(forward)
    sends[2].wait_recv()
    sends[3].wait_recv()
    for index, slot in ((0, 3), (1, 4)):
        part = store.at[pl.ds(slot * UNITS + (1 - core) * HALF, HALF)]
        remote(part, part, 4 + index, 4 + index, me + 1 - 2 * core).wait_recv()

    lat_sends = [
        remote(lat.at[pl.ds(512, 512)], lat.at[pl.ds(1536, 512)], 6, 6, me - 1),
        remote(lat.at[pl.ds(1024, 512)], lat.at[pl.ds(0, 512)], 7, 7, me + 1),
    ]
    for copy in lat_sends:
        copy.start()

    lane = lax.broadcasted_iota(jnp.int32, (32, 128), 1)
    low_x = lane < 64
    low_y = (lane // 8 % 8 == 7, lane < 48)
    low_z = ((lane % 8 == 7), ((lane < 96) & (lane % 8 == 7)) | ((lane >= 96) & (lane < 112)))
    third = lane // 40
    first_extra = lane % 40 < 20

    def pick(b, carry):
        rows = pl.ds(b * 32, 32)
        tiles = []
        for face in range(6):
            peer = nbr_ref[face, b]
            rel = peer // 16 - 2 * chip
            slot = jnp.where(
                rel == 0, 0, jnp.where(rel == 1, 1, jnp.where(rel == -1, 3, jnp.where(rel == 2, 4, 2)))
            )
            start = jnp.where(peer >= 0, slot, 5) * UNITS
            brick = jnp.where(peer >= 0, peer % 16, 0)
            own_third = jnp.where(brick >= 12, 2, jnp.where(brick >= 6, 1, 0))
            found = [store[start + brick]]
            if face >= 2:
                found.append(store[start + 16 + brick])
            if face >= 4:
                extra = store[start + 32 + brick - 6 * own_third]
                mine = (third == own_third) & (first_extra if face == 4 else jnp.logical_not(first_extra))
                found.append(jnp.where(mine, extra, jnp.zeros_like(extra)))
            tiles.append(found)
        picked = [jnp.where(low_y[t], tiles[2][t], tiles[3][t]) for t in range(2)]
        picked.append(jnp.where(low_x, tiles[0][0], tiles[1][0]))
        picked += [jnp.where(low_z[t], tiles[4][t], tiles[5][t]) for t in range(2)]
        picked.append(tiles[4][2] + tiles[5][2])
        for index, tile in enumerate(picked):
            ghosts[rows, pl.ds(index * 128, 128)] = tile
        return carry

    lax.fori_loop(0, 16, pick, 0)

    inner = pl.ds(1, 4)
    for g in range(2):
        rows = pl.ds(g * 256, 256)

        def ghost_part(start, count, lanes):
            return dot_nt(ghost_t[pl.ds(start, count), lanes], ghosts[rows, lanes]).astype(BF)

        for index, i in enumerate((0, 3)):
            part = ghost_part(index * 256, 256, pl.ds(256, 128)).reshape(4, 4, 16, 256)
            slabs[g, i, inner, inner] = slabs[g, i, inner, inner] + part
        for index, j in enumerate((0, 5)):
            part = ghost_part(512 + index * 384, 384, pl.ds(0, 768)).reshape(4, 6, 16, 256)
            slabs[g, :, j] = slabs[g, :, j] + part
        for index, k in enumerate((0, 5)):
            part = ghost_part(1280 + index * 256, 256, pl.ds(256, 512)).reshape(4, 4, 16, 256)
            slabs[g, :, inner, k] = slabs[g, :, inner, k] + part

    def conv_group(g, carry):
        total = jnp.zeros((256, 512), F32)
        for tap in range(27):
            i, j, k = tap // 9, tap // 3 % 3, tap % 3
            patch = slabs[g, pl.ds(i, 2), pl.ds(j, 4), pl.ds(k, 4)].reshape(512, 256)
            total = total + dot_nt(block_w[tap], patch)
        rows = pl.ds(pl.multiple_of(g * 256, 256), 256)
        conv_s[rows, :] = total
        return carry

    lax.fori_loop(0, 2, conv_group, 0)
    for g in range(2):
        parts = []
        for b in range(8):
            rows = pl.ds(g * 256 + b * 32, 32)
            pre = conv_s[rows, :] + bias_col
            mixed = masked_s[rows, :].astype(F32) + pre / (1.0 + jnp.exp(-pre))
            parts.append(jnp.where(occ_ref[g * 8 + b] > 0, mixed, 0.0).astype(BF))
        conv_g = jnp.concatenate(parts, axis=0)
        pooled[1 + g, pl.ds(0, 64), :] = dot_nt(pool_t[...], conv_g).astype(BF)
        masked_s[pl.ds(g * 256, 256), :] = conv_g

    pool_sends = [
        remote(pooled.at[1], pooled.at[3], 8, 8, me - 1),
        remote(pooled.at[2], pooled.at[0], 9, 9, me + 1),
    ]
    for copy in pool_sends:
        copy.start()
    conv_out_ref[...] = dot(masked_s[...], order_t[...]).astype(BF)

    wide_row = lax.broadcasted_iota(jnp.int32, (512, 256), 0)
    wide_lane = lax.broadcasted_iota(jnp.int32, (512, 256), 1)
    same_brick = wide_row // 64 == wide_lane // 32
    first_lane = same_brick & (wide_lane % 32 == 0)
    def project(g):
        cells = pooled[g, pl.ds(0, 64), :]
        tall = jnp.concatenate([cells] * 8, axis=0)
        tall = jnp.where(same_brick, tall, jnp.zeros_like(tall))
        latent = lat[pl.ds(g * 512, 512), :]
        mixed = latent.astype(F32) + dot(tall, proj_tile)
        scale = lax.rsqrt(jnp.mean(mixed * mixed, axis=-1, keepdims=True) + 1e-06)
        normed = (mixed * scale * gain_ref[...]).astype(BF)
        k_all = dot(normed, qkv_w[1]).astype(BF)
        for pair in range(4):
            keys[pair, pl.ds(g * 512, 512), :] = k_all[:, pair * 128 : pair * 128 + 128]
        v_all = dot_nt(vw_t[...], normed).astype(BF)
        for h in range(8):
            vals[h, pl.ds(0, 64), pl.ds(g * 512, 512)] = v_all[h * 64 : h * 64 + 64]
        if g in (1, 2):
            lanes = pl.ds((g - 1) * 512, 512)
            q_all = (dot_nt(qw_t[...], normed) * Q_SCALE).astype(BF)
            for h in range(8):
                qry[h, pl.ds(64 * (h % 2), 64), lanes] = q_all[h * 64 : h * 64 + 64]
            base_t[:, lanes] = dot_nt(eye, latent) + dot_nt(proj_t[...], tall)
        else:
            alive = jnp.broadcast_to(pooled[g, pl.ds(64, 16), :][:1], (128, 256))
            level = dot_nt(first_lane.astype(F32).astype(BF), alive)
            level = jnp.where(level > 0.5, 0.0, NEG)
            mask[1, g // 3] = jnp.concatenate([level] * 4, axis=1)

    def score_chunk(side, half, pair, h, chunk, dst):
        rows = pl.ds(chunk * 256, 256)
        base = 512 + half * 512 if side == 0 else half * 1536
        part = dot(keys[pair, pl.ds(base + chunk * 256, 256), :], qry[h, :, pl.ds(half * 512, 512)])
        part = part + mask[side, half, rows, :]
        dst[rows, :] = part
        return jnp.max(part.reshape(32, 8, 512), axis=0)

    def head_step(side, half, h, now, peaks, nxt, n_half, n_pair, n_head):
        lanes = pl.ds(half * 512, 512)
        base = 512 + half * 512 if side == 0 else half * 1536
        peak = jnp.max(peaks, axis=0, keepdims=True)
        if side == 1:
            own_peak = parts_s[h, pl.ds(72, 8), lanes][:1]
            peak = jnp.maximum(peak, own_peak)
        new_peaks, total = None, None
        for chunk in range(2):
            if nxt is not None:
                top = score_chunk(side, n_half, n_pair, n_head, chunk, nxt)
                new_peaks = top if chunk == 0 else jnp.maximum(new_peaks, top)
            weights = jnp.exp2(now[pl.ds(chunk * 256, 256), :] - peak).astype(BF)
            part = dot(vals[h, :, pl.ds(base + chunk * 256, 256)], weights)
            total = part if chunk == 0 else total + part
        if side == 0:
            parts_s[h, pl.ds(0, 72), lanes] = total[:72]
            parts_s[h, pl.ds(72, 8), lanes] = jnp.broadcast_to(peak, (8, 512))
        else:
            total = total[:72] + parts_s[h, pl.ds(0, 72), lanes] * jnp.exp2(own_peak - peak)
            out = (total[:64] / total[64:65]).astype(BF)
            att[pl.ds(pl.multiple_of(h * 64, 64), 64), lanes] = out
        return new_peaks

    def attend(side):
        peaks = None
        for chunk in range(2):
            top = score_chunk(side, 0, 0, 0, chunk, even_s)
            peaks = top if chunk == 0 else jnp.maximum(peaks, top)
        for half in range(2):

            def pair_step(pair, tops):
                tops = head_step(side, half, pair * 2, even_s, tops, odd_s, half, pair, pair * 2 + 1)
                return head_step(side, half, pair * 2 + 1, odd_s, tops, even_s, half, pair + 1, pair * 2 + 2)

            peaks = lax.fori_loop(0, 3, pair_step, peaks)
            peaks = head_step(side, half, 6, even_s, peaks, odd_s, half, 3, 7)
            peaks = head_step(side, half, 7, odd_s, peaks, even_s if half == 0 else None, 1, 0, 0)
            if side == 1:
                lanes = pl.ds(half * 512, 512)
                tokens_ref[:, lanes] = (base_t[:, lanes] + dot(ow_t[...], att[:, lanes])).astype(BF)

    project(1)
    project(2)
    attend(0)
    for copy in lat_sends + pool_sends:
        copy.wait_recv()
    project(0)
    project(3)
    attend(1)

    for copy in sends + forwards + lat_sends + pool_sends:
        copy.wait_send()


def local(n_space, n_chan, features, occupancy, neighbours, conv_weight, conv_bias, latent, token_proj, norm_gain, qkv_weight, out_weight):
    tables = slab_tables()
    smem = pl.BlockSpec(memory_space=pltpu.SMEM)
    vmem = pl.BlockSpec(memory_space=pltpu.VMEM)
    hbm = pl.BlockSpec(memory_space=pl.ANY)
    conv_out, tokens_out = pl.pallas_call(
        functools.partial(kernel, n_space, n_chan),
        out_shape=(pltpu.VMEM((512, 512), BF), pltpu.VMEM((512, 1024), BF)),
        in_specs=[smem, smem, vmem, vmem, vmem] + [hbm] * 11,
        out_specs=(vmem, vmem),
        scratch_shapes=[
            pltpu.VMEM((512, 512), BF),
            pltpu.VMEM((27, 32, 32), BF),
            pltpu.VMEM((2048, 512), BF),
            pltpu.VMEM((3, 512, 512), BF),
            pltpu.VMEM((512, 512), BF),
            pltpu.VMEM((ROWS, 512), BF),
            pltpu.VMEM((GHOST_ROWS, 768), BF),
            pltpu.VMEM((512, 256), BF),
            pltpu.VMEM((3, 512, 128), BF),
            pltpu.VMEM((512, 512), BF),
            pltpu.VMEM((64, 512), BF),
            pltpu.VMEM((6 * UNITS, 32, 128), BF),
            pltpu.VMEM((512, 768), BF),
            pltpu.VMEM((2,) + SLABS + (16, 256), BF),
            pltpu.VMEM((27, 256, 256), BF),
            pltpu.VMEM((512, 512), BF),
            pltpu.VMEM((512, 512), F32),
            pltpu.VMEM((4, 80, 256), BF),
            pltpu.VMEM((512, 256), BF),
            pltpu.VMEM((512, 512), BF),
            pltpu.VMEM((512, 512), BF),
            pltpu.VMEM((512, 512), BF),
            pltpu.VMEM((512, 1024), F32),
            pltpu.VMEM((2, 2, 512, 512), F32),
            pltpu.VMEM((4, 2048, 128), BF),
            pltpu.VMEM((8, 80, 2048), BF),
            pltpu.VMEM((8, 128, 1024), BF),
            pltpu.VMEM((512, 1024), BF),
            pltpu.VMEM((512, 512), F32),
            pltpu.VMEM((512, 512), F32),
            pltpu.VMEM((8, 80, 1024), F32),
            pltpu.SemaphoreType.DMA((11,)),
            pltpu.SemaphoreType.DMA((10,)),
            pltpu.SemaphoreType.DMA((10,)),
        ],
        compiler_params=pltpu.CompilerParams(
            collective_id=0, has_side_effects=True, vmem_limit_bytes=60 * 1024 * 1024
        ),
        cost_estimate=pl.CostEstimate(flops=8 * 10**9, bytes_accessed=12 * 10**6, transcendentals=9 * 10**6),
    )(
        occupancy,
        neighbours.T,
        conv_bias.reshape(1, 32),
        norm_gain.reshape(1, 512),
        token_proj,
        features.reshape(512, 512),
        conv_weight,
        latent,
        qkv_weight,
        out_weight,
        *tables,
    )
    return conv_out.reshape(16, 32, 512), tokens_out


def solution(mesh):
    both = ("space", "chan")
    return jax.shard_map(
        functools.partial(local, mesh.shape["space"], mesh.shape["chan"]),
        mesh=mesh,
        in_specs=(
            P(both, None, None),
            P(both),
            P(both, None),
            P(),
            P(),
            P(both, None),
            P(),
            P(),
            P(),
            P(),
        ),
        out_specs=(P(both, None, None), P(None, both)),
        check_vma=False,
    )
```

```python
import functools

import jax
import jax.numpy as jnp
import numpy as np
from jax import lax
from jax.experimental import pallas as pl
from jax.experimental.pallas import tpu as pltpu
from jax.sharding import PartitionSpec as P

MESH = pl.DeviceIdType.MESH
BF = jnp.bfloat16
F32 = jnp.float32
NEG = -1e30
SLABS = (4, 6, 6)
ROWS = 144 * 16
GHOST_ROWS = 1792
UNITS = 38
HALF = 19
Q_SCALE = 0.125 * 1.4426950408889634


def shell_lane(x, y, z):
    if x in (0, 7):
        return (0 if x == 7 else 64) + 8 * y + z, False
    if y in (0, 7):
        return 128 + (0 if y == 7 else 48) + 8 * (x - 1) + z, False
    index = 6 * (x - 1) + y - 1
    if index < 16:
        return 128 + (96 if z == 7 else 112) + index, False
    return (0 if z == 7 else 20) + index - 16, True


def slab_tables():
    i, j, k, xh, yh, zh = np.meshgrid(
        np.arange(4), np.arange(6), np.arange(6), np.arange(4), np.arange(2), np.arange(2), indexing="ij"
    )
    x, y, z = (2 * xh + i - 1).ravel(), (4 * yh + j - 1).ravel(), (4 * zh + k - 1).ravel()
    inside = [(c >= 0) & (c < 8) for c in (x, y, z)]
    row = np.arange(ROWS)
    voxel_rows = np.zeros((ROWS, 512), np.float32)
    hit = inside[0] & inside[1] & inside[2]
    voxel_rows[row[hit], (64 * x + 8 * y + z)[hit]] = 1
    ghost_rows = np.zeros((ROWS, 768), np.float32)
    for r in range(ROWS):
        cell = (int(x[r]), int(y[r]), int(z[r]))
        out = [a for a in range(3) if not inside[a][r]]
        if len(out) != 1:
            continue
        axis = out[0]
        source = tuple((c % 8) if a == axis else c for a, c in enumerate(cell))
        lane, extra = shell_lane(*source)
        if extra:
            ghost_rows[r, [640 + 40 * third + lane for third in range(3)]] = 1
        else:
            ghost_rows[r, (256, 0, 384)[axis] + lane] = 1
    by_slab = ghost_rows.reshape(4, 6, 6, 16, 768)
    parts = [by_slab[i, 1:5, 1:5] for i in (0, 3)] + [by_slab[:, j] for j in (0, 5)] + [by_slab[:, 1:5, k] for k in (0, 5)]
    ghost_rows = np.concatenate([part.reshape(-1, 768) for part in parts])
    faces = np.zeros((512, 256), np.float32)
    extras = np.zeros((3, 512, 128), np.float32)
    for vx, vy, vz in np.ndindex(8, 8, 8):
        if min(vx, vy, vz) > 0 and max(vx, vy, vz) < 7:
            continue
        lane, extra = shell_lane(vx, vy, vz)
        voxel = 64 * vx + 8 * vy + vz
        if extra:
            for third in range(3):
                extras[third, voxel, 40 * third + lane] = 1
        else:
            faces[voxel, lane] = 1
    xl, yl, zl, xh, yh, zh = [
        a.ravel()
        for a in np.meshgrid(*[np.arange(n) for n in (2, 4, 4, 4, 2, 2)], indexing="ij")
    ]
    x, y, z = 2 * xh + xl, 4 * yh + yl, 4 * zh + zl
    order = np.zeros((512, 512), np.float32)
    order[np.arange(512), 64 * x + 8 * y + z] = 1
    p, q, r = x // 2, y // 2, z // 2
    token = 32 * (p // 2) + 16 * (q // 2) + 8 * (r // 2) + 4 * (p % 2) + 2 * (q % 2) + r % 2
    pool = np.zeros((64, 512), np.float32)
    pool[token, np.arange(512)] = 0.125
    return [jnp.asarray(t, BF) for t in (voxel_rows, ghost_rows, faces, extras, order, pool)]


def dot(a, b):
    return lax.dot_general(a, b, (((1,), (0,)), ((), ())), preferred_element_type=F32)


def dot_nt(a, b):
    return lax.dot_general(a, b, (((1,), (1,)), ((), ())), preferred_element_type=F32)


def kernel(
    n_space,
    n_chan,
    occ_ref,
    nbr_ref,
    bias_ref,
    gain_ref,
    proj_ref,
    feat_hbm,
    conv_w_hbm,
    latent_hbm,
    qkv_hbm,
    out_w_hbm,
    vox_hbm,
    ghost_hbm,
    face_hbm,
    extra_hbm,
    order_hbm,
    pool_hbm,
    conv_out_ref,
    tokens_ref,
    feat,
    conv_w,
    lat,
    qkv_w,
    out_w,
    vox_t,
    ghost_t,
    face_t,
    extra_t,
    order_t,
    pool_t,
    store,
    ghosts,
    slabs,
    block_w,
    masked_s,
    conv_s,
    pooled,
    proj_t,
    qw_t,
    vw_t,
    ow_t,
    base_t,
    mask,
    keys,
    vals,
    qry,
    att,
    even_s,
    odd_s,
    parts_s,
    lat_k,
    lat_v,
    lat_q,
    proj_k,
    proj_v,
    proj_q,
    load_sem,
    send_sem,
    recv_sem,
):
    count = n_space * n_chan
    me = lax.axis_index("space") * n_chan + lax.axis_index("chan")
    core = me % 2
    chip = me // 2

    def place(index):
        index = (index + count) % count
        return (index // n_chan, index % n_chan)

    barrier = pltpu.get_barrier_semaphore()
    for step in (-2, -1, 1, 2):
        pl.semaphore_signal(barrier, inc=1, device_id=place(me + step), device_id_type=MESH)

    loads = {}
    for index, (name, src, dst) in enumerate(
        (
            ("feat", feat_hbm, feat),
            ("face", face_hbm, face_t),
            ("extra", extra_hbm, extra_t),
            ("vox", vox_hbm, vox_t),
            ("order", order_hbm, order_t),
            ("conv_w", conv_w_hbm, conv_w),
            ("ghost", ghost_hbm, ghost_t),
            ("lat", latent_hbm, lat.at[pl.ds(512, 1024)]),
            ("qkv", qkv_hbm, qkv_w),
            ("out_w", out_w_hbm, out_w),
            ("pool", pool_hbm, pool_t),
        )
    ):
        loads[name] = pltpu.make_async_copy(src, dst, load_sem.at[index])
        loads[name].start()

    def remote(src, dst, send, recv, target):
        return pltpu.make_async_remote_copy(
            src_ref=src,
            dst_ref=dst,
            send_sem=send_sem.at[send],
            recv_sem=recv_sem.at[recv],
            device_id=place(target),
            device_id_type=MESH,
        )

    loads["feat"].wait()
    for b in range(16):
        rows = pl.ds(b * 32, 32)
        block = feat[rows, :]
        feat[rows, :] = jnp.where(occ_ref[b] > 0, block, jnp.zeros_like(block))
    loads["face"].wait()
    own_start = core * UNITS
    for tile in range(2):
        cells = dot(feat[...], face_t[:, pl.ds(tile * 128, 128)]).astype(BF)
        store[pl.ds(own_start + tile * 16, 16)] = cells.reshape(16, 32, 128)
    loads["extra"].wait()
    packed = [dot(feat[pl.ds(192 * t, 192 if t < 2 else 128), :], extra_t[t]) for t in range(3)]
    packed = packed[0] + packed[1] + jnp.concatenate([packed[2], jnp.zeros((64, 128), F32)], axis=0)
    store[pl.ds(own_start + 32, 6)] = packed.astype(BF).reshape(6, 32, 128)
    store[pl.ds(5 * UNITS, UNITS)] = jnp.zeros((UNITS, 32, 128), BF)

    pl.semaphore_wait(barrier, 4)
    own = store.at[pl.ds(own_start, UNITS)]
    shared_slot = 4 - core
    shared_base = 2 * (chip - 1) + 4 * core
    sends = []
    for half in range(2):
        sends.append(
            remote(
                store.at[pl.ds(own_start + half * HALF, HALF)],
                store.at[pl.ds(shared_slot * UNITS + half * HALF, HALF)],
                half,
                1 - core,
                shared_base + half,
            )
        )
    sends.append(remote(own, own, 2, 2, me + 1 - 2 * core))
    sends.append(remote(own, store.at[pl.ds(2 * UNITS, UNITS)], 3, 3, me + 2 - 4 * core))
    for copy in sends:
        copy.start()

    loads["vox"].wait()
    for g in range(2):
        block = feat[pl.ds(g * 256, 256), :]
        for i in range(4):
            part = dot_nt(vox_t[pl.ds(i * 576, 576), :], block).astype(BF)
            slabs[g, i] = part.reshape(6, 6, 16, 256)
    loads["order"].wait()
    masked_s[...] = dot_nt(feat[...], order_t[...]).astype(BF)

    loads["conv_w"].wait()
    rep_row = lax.broadcasted_iota(jnp.int32, (32, 256), 0)
    rep_lane = lax.broadcasted_iota(jnp.int32, (32, 256), 1)
    spread = (rep_lane % 32 == rep_row).astype(F32).astype(BF)

    def block_tap(tap, carry):
        wide = dot(conv_w[tap], spread).astype(BF)
        for b in range(8):
            block_w[tap, pl.ds(b * 32, 32), :] = jnp.where(rep_lane // 32 == b, wide, jnp.zeros_like(wide))
        return carry

    lax.fori_loop(0, 27, block_tap, 0)

    eye_row = lax.broadcasted_iota(jnp.int32, (512, 512), 0)
    eye_lane = lax.broadcasted_iota(jnp.int32, (512, 512), 1)
    eye = (eye_row == eye_lane).astype(F32).astype(BF)
    loads["qkv"].wait()
    loads["out_w"].wait()
    qw_t[...] = dot_nt(eye, qkv_w[0]).astype(BF)
    vw_t[...] = dot_nt(eye, qkv_w[2]).astype(BF)
    ow_t[...] = dot_nt(eye, out_w[...]).astype(BF)
    proj_tile = jnp.concatenate([proj_ref[...]] * 8, axis=0)
    proj_t[...] = dot_nt(eye, proj_tile).astype(BF)

    small_row = lax.broadcasted_iota(jnp.int32, (32, 32), 0)
    small_lane = lax.broadcasted_iota(jnp.int32, (32, 32), 1)
    bias_col = jnp.sum(jnp.where(small_row == small_lane, bias_ref[...], 0.0), axis=1, keepdims=True)

    m_row = lax.broadcasted_iota(jnp.int32, (64, 512), 0)
    m_lane = lax.broadcasted_iota(jnp.int32, (64, 512), 1)
    for b in range(16):
        half, slot = b // 8, b % 8
        level = jnp.where(occ_ref[b] > 0, 0.0, NEG)
        mask[0, half, pl.ds(slot * 64, 64), :] = jnp.where(m_row + slot * 64 == m_lane, 0.0, level)

    occ_lane = lax.broadcasted_iota(jnp.int32, (16, 256), 1) // 32
    for g in range(2):
        row = jnp.zeros((16, 256), F32)
        for b in range(8):
            row = jnp.where(occ_lane == b, occ_ref[g * 8 + b].astype(F32), row)
        pooled[1 + g, pl.ds(64, 16), :] = row.astype(BF)

    for h in range(8):
        vals[h, pl.ds(64, 16), :] = jnp.ones((16, 2048), BF)
        qry[h, pl.ds(64 * (1 - h % 2), 64), :] = jnp.zeros((64, 1024), BF)

    loads["ghost"].wait()
    loads["pool"].wait()
    loads["lat"].wait()

    gained_proj = (proj_tile.astype(F32) * gain_ref[...]).astype(BF)
    proj_k[...] = dot(gained_proj, qkv_w[1]).astype(BF)
    proj_v[...] = dot_nt(vw_t[...], gained_proj).astype(BF)
    proj_q[...] = dot_nt(qw_t[...], gained_proj).astype(BF)
    for half in range(2):
        tokens = pl.ds(half * 512, 512)
        latent = lat[pl.ds(512 + half * 512, 512), :]
        gained = (latent.astype(F32) * gain_ref[...]).astype(BF)
        lat_k[tokens, :] = dot(gained, qkv_w[1])
        lat_v[:, tokens] = dot_nt(vw_t[...], gained)
        lat_q[:, tokens] = dot_nt(qw_t[...], gained)
        base_t[:, tokens] = dot_nt(eye, latent)

    forwards = []
    for index, slot in ((0, 3), (1, 4)):
        part = store.at[pl.ds(slot * UNITS + core * HALF, HALF)]
        remote(part, part, 4 + index, index, me + 1 - 2 * core).wait_recv()
        forward = remote(part, part, 4 + index, 4 + index, me + 1 - 2 * core)
        forward.start()
        forwards.append(forward)
    sends[2].wait_recv()
    sends[3].wait_recv()
    for index, slot in ((0, 3), (1, 4)):
        part = store.at[pl.ds(slot * UNITS + (1 - core) * HALF, HALF)]
        remote(part, part, 4 + index, 4 + index, me + 1 - 2 * core).wait_recv()

    lat_sends = [
        remote(lat.at[pl.ds(512, 512)], lat.at[pl.ds(1536, 512)], 6, 6, me - 1),
        remote(lat.at[pl.ds(1024, 512)], lat.at[pl.ds(0, 512)], 7, 7, me + 1),
    ]
    for copy in lat_sends:
        copy.start()

    lane = lax.broadcasted_iota(jnp.int32, (32, 128), 1)
    low_x = lane < 64
    low_y = (lane // 8 % 8 == 7, lane < 48)
    low_z = ((lane % 8 == 7), ((lane < 96) & (lane % 8 == 7)) | ((lane >= 96) & (lane < 112)))
    third = lane // 40
    first_extra = lane % 40 < 20

    def pick(b, carry):
        rows = pl.ds(b * 32, 32)
        tiles = []
        for face in range(6):
            peer = nbr_ref[face, b]
            rel = peer // 16 - 2 * chip
            slot = jnp.where(
                rel == 0, 0, jnp.where(rel == 1, 1, jnp.where(rel == -1, 3, jnp.where(rel == 2, 4, 2)))
            )
            start = jnp.where(peer >= 0, slot, 5) * UNITS
            brick = jnp.where(peer >= 0, peer % 16, 0)
            own_third = jnp.where(brick >= 12, 2, jnp.where(brick >= 6, 1, 0))
            found = [store[start + brick]]
            if face >= 2:
                found.append(store[start + 16 + brick])
            if face >= 4:
                extra = store[start + 32 + brick - 6 * own_third]
                mine = (third == own_third) & (first_extra if face == 4 else jnp.logical_not(first_extra))
                found.append(jnp.where(mine, extra, jnp.zeros_like(extra)))
            tiles.append(found)
        picked = [jnp.where(low_y[t], tiles[2][t], tiles[3][t]) for t in range(2)]
        picked.append(jnp.where(low_x, tiles[0][0], tiles[1][0]))
        picked += [jnp.where(low_z[t], tiles[4][t], tiles[5][t]) for t in range(2)]
        picked.append(tiles[4][2] + tiles[5][2])
        for index, tile in enumerate(picked):
            ghosts[rows, pl.ds(index * 128, 128)] = tile
        return carry

    lax.fori_loop(0, 16, pick, 0)

    inner = pl.ds(1, 4)
    for g in range(2):
        rows = pl.ds(g * 256, 256)

        def ghost_part(start, count, lanes):
            return dot_nt(ghost_t[pl.ds(start, count), lanes], ghosts[rows, lanes]).astype(BF)

        for index, i in enumerate((0, 3)):
            part = ghost_part(index * 256, 256, pl.ds(256, 128)).reshape(4, 4, 16, 256)
            slabs[g, i, inner, inner] = slabs[g, i, inner, inner] + part
        for index, j in enumerate((0, 5)):
            part = ghost_part(512 + index * 384, 384, pl.ds(0, 768)).reshape(4, 6, 16, 256)
            slabs[g, :, j] = slabs[g, :, j] + part
        for index, k in enumerate((0, 5)):
            part = ghost_part(1280 + index * 256, 256, pl.ds(256, 512)).reshape(4, 4, 16, 256)
            slabs[g, :, inner, k] = slabs[g, :, inner, k] + part

    def conv_group(g, carry):
        total = jnp.zeros((256, 512), F32)
        for tap in range(27):
            i, j, k = tap // 9, tap // 3 % 3, tap % 3
            patch = slabs[g, pl.ds(i, 2), pl.ds(j, 4), pl.ds(k, 4)].reshape(512, 256)
            total = total + dot_nt(block_w[tap], patch)
        rows = pl.ds(pl.multiple_of(g * 256, 256), 256)
        conv_s[rows, :] = total
        return carry

    lax.fori_loop(0, 2, conv_group, 0)
    for g in range(2):
        parts = []
        for b in range(8):
            rows = pl.ds(g * 256 + b * 32, 32)
            pre = conv_s[rows, :] + bias_col
            mixed = masked_s[rows, :].astype(F32) + pre / (1.0 + jnp.exp(-pre))
            parts.append(jnp.where(occ_ref[g * 8 + b] > 0, mixed, 0.0).astype(BF))
        conv_g = jnp.concatenate(parts, axis=0)
        pooled[1 + g, pl.ds(0, 64), :] = dot_nt(pool_t[...], conv_g).astype(BF)
        masked_s[pl.ds(g * 256, 256), :] = conv_g

    pool_sends = [
        remote(pooled.at[1], pooled.at[3], 8, 8, me - 1),
        remote(pooled.at[2], pooled.at[0], 9, 9, me + 1),
    ]
    for copy in pool_sends:
        copy.start()
    conv_out_ref[...] = dot(masked_s[...], order_t[...]).astype(BF)

    wide_row = lax.broadcasted_iota(jnp.int32, (512, 256), 0)
    wide_lane = lax.broadcasted_iota(jnp.int32, (512, 256), 1)
    same_brick = wide_row // 64 == wide_lane // 32
    first_lane = same_brick & (wide_lane % 32 == 0)
    def project(g):
        cells = pooled[g, pl.ds(0, 64), :]
        tall = jnp.concatenate([cells] * 8, axis=0)
        tall = jnp.where(same_brick, tall, jnp.zeros_like(tall))
        latent = lat[pl.ds(g * 512, 512), :]
        mixed = latent.astype(F32) + dot(tall, proj_tile)
        scale = lax.rsqrt(jnp.mean(mixed * mixed, axis=-1, keepdims=True) + 1e-06)
        if g in (1, 2):
            lanes = pl.ds((g - 1) * 512, 512)
            whole = base_t[:, lanes] + dot_nt(proj_t[...], tall)
            base_t[:, lanes] = whole
            scale_row = lax.rsqrt(jnp.mean(whole * whole, axis=0, keepdims=True) + 1e-06)
            k_all = ((lat_k[lanes, :] + dot(tall, proj_k[...])) * scale).astype(BF)
            v_all = ((lat_v[:, lanes] + dot_nt(proj_v[...], tall)) * scale_row).astype(BF)
            q_all = ((lat_q[:, lanes] + dot_nt(proj_q[...], tall)) * (scale_row * Q_SCALE)).astype(BF)
            for h in range(8):
                qry[h, pl.ds(64 * (h % 2), 64), lanes] = q_all[h * 64 : h * 64 + 64]
        else:
            normed = (mixed * scale * gain_ref[...]).astype(BF)
            k_all = dot(normed, qkv_w[1]).astype(BF)
            v_all = dot_nt(vw_t[...], normed).astype(BF)
            alive = jnp.broadcast_to(pooled[g, pl.ds(64, 16), :][:1], (128, 256))
            level = dot_nt(first_lane.astype(F32).astype(BF), alive)
            level = jnp.where(level > 0.5, 0.0, NEG)
            mask[1, g // 3] = jnp.concatenate([level] * 4, axis=1)
        for pair in range(4):
            keys[pair, pl.ds(g * 512, 512), :] = k_all[:, pair * 128 : pair * 128 + 128]
        for h in range(8):
            vals[h, pl.ds(0, 64), pl.ds(g * 512, 512)] = v_all[h * 64 : h * 64 + 64]

    def score_chunk(side, half, pair, h, chunk, dst):
        rows = pl.ds(chunk * 256, 256)
        base = 512 + half * 512 if side == 0 else half * 1536
        part = dot(keys[pair, pl.ds(base + chunk * 256, 256), :], qry[h, :, pl.ds(half * 512, 512)])
        part = part + mask[side, half, rows, :]
        dst[rows, :] = part
        return jnp.max(part.reshape(32, 8, 512), axis=0)

    def head_step(side, half, h, now, peaks, nxt, n_half, n_pair, n_head):
        lanes = pl.ds(half * 512, 512)
        base = 512 + half * 512 if side == 0 else half * 1536
        peak = jnp.max(peaks, axis=0, keepdims=True)
        if side == 1:
            own_peak = parts_s[h, pl.ds(72, 8), lanes][:1]
            peak = jnp.maximum(peak, own_peak)
        new_peaks, total = None, None
        for chunk in range(2):
            if nxt is not None:
                top = score_chunk(side, n_half, n_pair, n_head, chunk, nxt)
                new_peaks = top if chunk == 0 else jnp.maximum(new_peaks, top)
            weights = jnp.exp2(now[pl.ds(chunk * 256, 256), :] - peak).astype(BF)
            part = dot(vals[h, :, pl.ds(base + chunk * 256, 256)], weights)
            total = part if chunk == 0 else total + part
        if side == 0:
            parts_s[h, pl.ds(0, 72), lanes] = total[:72]
            parts_s[h, pl.ds(72, 8), lanes] = jnp.broadcast_to(peak, (8, 512))
        else:
            total = total[:72] + parts_s[h, pl.ds(0, 72), lanes] * jnp.exp2(own_peak - peak)
            out = (total[:64] / total[64:65]).astype(BF)
            att[pl.ds(pl.multiple_of(h * 64, 64), 64), lanes] = out
        return new_peaks

    def attend(side):
        peaks = None
        for chunk in range(2):
            top = score_chunk(side, 0, 0, 0, chunk, even_s)
            peaks = top if chunk == 0 else jnp.maximum(peaks, top)
        for half in range(2):

            def pair_step(pair, tops):
                tops = head_step(side, half, pair * 2, even_s, tops, odd_s, half, pair, pair * 2 + 1)
                return head_step(side, half, pair * 2 + 1, odd_s, tops, even_s, half, pair + 1, pair * 2 + 2)

            peaks = lax.fori_loop(0, 3, pair_step, peaks)
            peaks = head_step(side, half, 6, even_s, peaks, odd_s, half, 3, 7)
            peaks = head_step(side, half, 7, odd_s, peaks, even_s if half == 0 else None, 1, 0, 0)
            if side == 1:
                lanes = pl.ds(half * 512, 512)
                tokens_ref[:, lanes] = (base_t[:, lanes] + dot(ow_t[...], att[:, lanes])).astype(BF)

    project(1)
    project(2)
    attend(0)
    for copy in lat_sends + pool_sends:
        copy.wait_recv()
    project(0)
    project(3)
    attend(1)

    for copy in sends + forwards + lat_sends + pool_sends:
        copy.wait_send()


def local(n_space, n_chan, features, occupancy, neighbours, conv_weight, conv_bias, latent, token_proj, norm_gain, qkv_weight, out_weight):
    tables = slab_tables()
    smem = pl.BlockSpec(memory_space=pltpu.SMEM)
    vmem = pl.BlockSpec(memory_space=pltpu.VMEM)
    hbm = pl.BlockSpec(memory_space=pl.ANY)
    conv_out, tokens_out = pl.pallas_call(
        functools.partial(kernel, n_space, n_chan),
        out_shape=(pltpu.VMEM((512, 512), BF), pltpu.VMEM((512, 1024), BF)),
        in_specs=[smem, smem, vmem, vmem, vmem] + [hbm] * 11,
        out_specs=(vmem, vmem),
        scratch_shapes=[
            pltpu.VMEM((512, 512), BF),
            pltpu.VMEM((27, 32, 32), BF),
            pltpu.VMEM((2048, 512), BF),
            pltpu.VMEM((3, 512, 512), BF),
            pltpu.VMEM((512, 512), BF),
            pltpu.VMEM((ROWS, 512), BF),
            pltpu.VMEM((GHOST_ROWS, 768), BF),
            pltpu.VMEM((512, 256), BF),
            pltpu.VMEM((3, 512, 128), BF),
            pltpu.VMEM((512, 512), BF),
            pltpu.VMEM((64, 512), BF),
            pltpu.VMEM((6 * UNITS, 32, 128), BF),
            pltpu.VMEM((512, 768), BF),
            pltpu.VMEM((2,) + SLABS + (16, 256), BF),
            pltpu.VMEM((27, 256, 256), BF),
            pltpu.VMEM((512, 512), BF),
            pltpu.VMEM((512, 512), F32),
            pltpu.VMEM((4, 80, 256), BF),
            pltpu.VMEM((512, 256), BF),
            pltpu.VMEM((512, 512), BF),
            pltpu.VMEM((512, 512), BF),
            pltpu.VMEM((512, 512), BF),
            pltpu.VMEM((512, 1024), F32),
            pltpu.VMEM((2, 2, 512, 512), F32),
            pltpu.VMEM((4, 2048, 128), BF),
            pltpu.VMEM((8, 80, 2048), BF),
            pltpu.VMEM((8, 128, 1024), BF),
            pltpu.VMEM((512, 1024), BF),
            pltpu.VMEM((512, 512), F32),
            pltpu.VMEM((512, 512), F32),
            pltpu.VMEM((8, 80, 1024), F32),
            pltpu.VMEM((1024, 512), F32),
            pltpu.VMEM((512, 1024), F32),
            pltpu.VMEM((512, 1024), F32),
            pltpu.VMEM((256, 512), BF),
            pltpu.VMEM((512, 256), BF),
            pltpu.VMEM((512, 256), BF),
            pltpu.SemaphoreType.DMA((11,)),
            pltpu.SemaphoreType.DMA((10,)),
            pltpu.SemaphoreType.DMA((10,)),
        ],
        compiler_params=pltpu.CompilerParams(
            collective_id=0, has_side_effects=True, vmem_limit_bytes=60 * 1024 * 1024
        ),
        cost_estimate=pl.CostEstimate(flops=8 * 10**9, bytes_accessed=12 * 10**6, transcendentals=9 * 10**6),
    )(
        occupancy,
        neighbours.T,
        conv_bias.reshape(1, 32),
        norm_gain.reshape(1, 512),
        token_proj,
        features.reshape(512, 512),
        conv_weight,
        latent,
        qkv_weight,
        out_weight,
        *tables,
    )
    return conv_out.reshape(16, 32, 512), tokens_out


def solution(mesh):
    both = ("space", "chan")
    return jax.shard_map(
        functools.partial(local, mesh.shape["space"], mesh.shape["chan"]),
        mesh=mesh,
        in_specs=(
            P(both, None, None),
            P(both),
            P(both, None),
            P(),
            P(),
            P(both, None),
            P(),
            P(),
            P(),
            P(),
        ),
        out_specs=(P(both, None, None), P(None, both)),
        check_vma=False,
    )
```

```python
import functools

import jax
import jax.numpy as jnp
import numpy as np
from jax import lax
from jax.experimental import pallas as pl
from jax.experimental.pallas import tpu as pltpu
from jax.sharding import PartitionSpec as P

MESH = pl.DeviceIdType.MESH
BF = jnp.bfloat16
F32 = jnp.float32
NEG = -1e30
SLABS = (4, 6, 6)
ROWS = 144 * 16
GHOST_ROWS = 1792
UNITS = 38
HALF = 19
Q_SCALE = 0.125 * 1.4426950408889634


def shell_lane(x, y, z):
    if x in (0, 7):
        return (0 if x == 7 else 64) + 8 * y + z, False
    if y in (0, 7):
        return 128 + (0 if y == 7 else 48) + 8 * (x - 1) + z, False
    index = 6 * (x - 1) + y - 1
    if index < 16:
        return 128 + (96 if z == 7 else 112) + index, False
    return (0 if z == 7 else 20) + index - 16, True


def slab_tables():
    i, j, k, xh, yh, zh = np.meshgrid(
        np.arange(4), np.arange(6), np.arange(6), np.arange(4), np.arange(2), np.arange(2), indexing="ij"
    )
    x, y, z = (2 * xh + i - 1).ravel(), (4 * yh + j - 1).ravel(), (4 * zh + k - 1).ravel()
    inside = [(c >= 0) & (c < 8) for c in (x, y, z)]
    row = np.arange(ROWS)
    voxel_rows = np.zeros((ROWS, 512), np.float32)
    hit = inside[0] & inside[1] & inside[2]
    voxel_rows[row[hit], (64 * x + 8 * y + z)[hit]] = 1
    ghost_rows = np.zeros((ROWS, 768), np.float32)
    for r in range(ROWS):
        cell = (int(x[r]), int(y[r]), int(z[r]))
        out = [a for a in range(3) if not inside[a][r]]
        if len(out) != 1:
            continue
        axis = out[0]
        source = tuple((c % 8) if a == axis else c for a, c in enumerate(cell))
        lane, extra = shell_lane(*source)
        if extra:
            ghost_rows[r, [640 + 40 * third + lane for third in range(3)]] = 1
        else:
            ghost_rows[r, (256, 0, 384)[axis] + lane] = 1
    by_slab = ghost_rows.reshape(4, 6, 6, 16, 768)
    parts = [by_slab[i, 1:5, 1:5] for i in (0, 3)] + [by_slab[:, j] for j in (0, 5)] + [by_slab[:, 1:5, k] for k in (0, 5)]
    ghost_rows = np.concatenate([part.reshape(-1, 768) for part in parts])
    faces = np.zeros((512, 256), np.float32)
    extras = np.zeros((3, 512, 128), np.float32)
    for vx, vy, vz in np.ndindex(8, 8, 8):
        if min(vx, vy, vz) > 0 and max(vx, vy, vz) < 7:
            continue
        lane, extra = shell_lane(vx, vy, vz)
        voxel = 64 * vx + 8 * vy + vz
        if extra:
            for third in range(3):
                extras[third, voxel, 40 * third + lane] = 1
        else:
            faces[voxel, lane] = 1
    xl, yl, zl, xh, yh, zh = [
        a.ravel()
        for a in np.meshgrid(*[np.arange(n) for n in (2, 4, 4, 4, 2, 2)], indexing="ij")
    ]
    x, y, z = 2 * xh + xl, 4 * yh + yl, 4 * zh + zl
    order = np.zeros((512, 512), np.float32)
    order[np.arange(512), 64 * x + 8 * y + z] = 1
    p, q, r = x // 2, y // 2, z // 2
    token = 32 * (p // 2) + 16 * (q // 2) + 8 * (r // 2) + 4 * (p % 2) + 2 * (q % 2) + r % 2
    pool = np.zeros((64, 512), np.float32)
    pool[token, np.arange(512)] = 0.125
    return [jnp.asarray(t, BF) for t in (voxel_rows, ghost_rows, faces, extras, order, pool)]


def dot(a, b):
    return lax.dot_general(a, b, (((1,), (0,)), ((), ())), preferred_element_type=F32)


def dot_nt(a, b):
    return lax.dot_general(a, b, (((1,), (1,)), ((), ())), preferred_element_type=F32)


def kernel(
    n_space,
    n_chan,
    occ_ref,
    nbr_ref,
    bias_ref,
    gain_ref,
    proj_ref,
    feat_hbm,
    conv_w_hbm,
    latent_hbm,
    qkv_hbm,
    out_w_hbm,
    vox_hbm,
    ghost_hbm,
    face_hbm,
    extra_hbm,
    order_hbm,
    pool_hbm,
    conv_out_ref,
    tokens_ref,
    feat,
    conv_w,
    lat,
    qkv_w,
    out_w,
    vox_t,
    ghost_t,
    face_t,
    extra_t,
    order_t,
    pool_t,
    store,
    ghosts,
    slabs,
    block_w,
    masked_s,
    conv_s,
    pooled,
    proj_t,
    qw_t,
    vw_t,
    ow_t,
    base_t,
    mask,
    keys,
    vals,
    qry,
    att,
    even_s,
    odd_s,
    parts_s,
    lat_k,
    lat_v,
    lat_q,
    proj_k,
    proj_v,
    proj_q,
    load_sem,
    send_sem,
    recv_sem,
):
    count = n_space * n_chan
    me = lax.axis_index("space") * n_chan + lax.axis_index("chan")
    core = me % 2
    chip = me // 2

    def place(index):
        index = (index + count) % count
        return (index // n_chan, index % n_chan)

    barrier = pltpu.get_barrier_semaphore()
    for step in (-2, -1, 1, 2):
        pl.semaphore_signal(barrier, inc=1, device_id=place(me + step), device_id_type=MESH)

    loads = {}
    for index, (name, src, dst) in enumerate(
        (
            ("feat", feat_hbm, feat),
            ("face", face_hbm, face_t),
            ("extra", extra_hbm, extra_t),
            ("vox", vox_hbm, vox_t),
            ("order", order_hbm, order_t),
            ("conv_w", conv_w_hbm, conv_w),
            ("ghost", ghost_hbm, ghost_t),
            ("lat", latent_hbm, lat.at[pl.ds(512, 1024)]),
            ("qkv", qkv_hbm, qkv_w),
            ("out_w", out_w_hbm, out_w),
            ("pool", pool_hbm, pool_t),
        )
    ):
        loads[name] = pltpu.make_async_copy(src, dst, load_sem.at[index])
        loads[name].start()

    def remote(src, dst, send, recv, target):
        return pltpu.make_async_remote_copy(
            src_ref=src,
            dst_ref=dst,
            send_sem=send_sem.at[send],
            recv_sem=recv_sem.at[recv],
            device_id=place(target),
            device_id_type=MESH,
        )

    loads["feat"].wait()
    for b in range(16):
        rows = pl.ds(b * 32, 32)
        block = feat[rows, :]
        feat[rows, :] = jnp.where(occ_ref[b] > 0, block, jnp.zeros_like(block))
    loads["face"].wait()
    own_start = core * UNITS
    for tile in range(2):
        cells = dot(feat[...], face_t[:, pl.ds(tile * 128, 128)]).astype(BF)
        store[pl.ds(own_start + tile * 16, 16)] = cells.reshape(16, 32, 128)
    loads["extra"].wait()
    packed = [dot(feat[pl.ds(192 * t, 192 if t < 2 else 128), :], extra_t[t]) for t in range(3)]
    packed = packed[0] + packed[1] + jnp.concatenate([packed[2], jnp.zeros((64, 128), F32)], axis=0)
    store[pl.ds(own_start + 32, 6)] = packed.astype(BF).reshape(6, 32, 128)
    store[pl.ds(5 * UNITS, UNITS)] = jnp.zeros((UNITS, 32, 128), BF)

    pl.semaphore_wait(barrier, 4)
    own = store.at[pl.ds(own_start, UNITS)]
    shared_slot = 4 - core
    shared_base = 2 * (chip - 1) + 4 * core
    sends = []
    for half in range(2):
        sends.append(
            remote(
                store.at[pl.ds(own_start + half * HALF, HALF)],
                store.at[pl.ds(shared_slot * UNITS + half * HALF, HALF)],
                half,
                1 - core,
                shared_base + half,
            )
        )
    sends.append(remote(own, own, 2, 2, me + 1 - 2 * core))
    sends.append(remote(own, store.at[pl.ds(2 * UNITS, UNITS)], 3, 3, me + 2 - 4 * core))
    for copy in sends:
        copy.start()

    loads["vox"].wait()
    for g in range(2):
        block = feat[pl.ds(g * 256, 256), :]
        for i in range(4):
            part = dot_nt(vox_t[pl.ds(i * 576, 576), :], block).astype(BF)
            slabs[g, i] = part.reshape(6, 6, 16, 256)
    loads["order"].wait()
    masked_s[...] = dot_nt(feat[...], order_t[...]).astype(BF)

    loads["conv_w"].wait()
    rep_row = lax.broadcasted_iota(jnp.int32, (32, 256), 0)
    rep_lane = lax.broadcasted_iota(jnp.int32, (32, 256), 1)
    spread = (rep_lane % 32 == rep_row).astype(F32).astype(BF)

    def block_tap(tap, carry):
        wide = dot(conv_w[tap], spread).astype(BF)
        for b in range(8):
            block_w[tap, pl.ds(b * 32, 32), :] = jnp.where(rep_lane // 32 == b, wide, jnp.zeros_like(wide))
        return carry

    lax.fori_loop(0, 27, block_tap, 0)

    eye_row = lax.broadcasted_iota(jnp.int32, (512, 512), 0)
    eye_lane = lax.broadcasted_iota(jnp.int32, (512, 512), 1)
    eye = (eye_row == eye_lane).astype(F32).astype(BF)
    loads["qkv"].wait()
    loads["out_w"].wait()
    qw_t[...] = dot_nt(eye, qkv_w[0]).astype(BF)
    vw_t[...] = dot_nt(eye, qkv_w[2]).astype(BF)
    ow_t[...] = dot_nt(eye, out_w[...]).astype(BF)
    proj_tile = jnp.concatenate([proj_ref[...]] * 8, axis=0)
    proj_t[...] = dot_nt(eye, proj_tile).astype(BF)

    small_row = lax.broadcasted_iota(jnp.int32, (32, 32), 0)
    small_lane = lax.broadcasted_iota(jnp.int32, (32, 32), 1)
    bias_col = jnp.sum(jnp.where(small_row == small_lane, bias_ref[...], 0.0), axis=1, keepdims=True)

    m_row = lax.broadcasted_iota(jnp.int32, (64, 512), 0)
    m_lane = lax.broadcasted_iota(jnp.int32, (64, 512), 1)
    for b in range(16):
        half, slot = b // 8, b % 8
        level = jnp.where(occ_ref[b] > 0, 0.0, NEG)
        mask[0, half, pl.ds(slot * 64, 64), :] = jnp.where(m_row + slot * 64 == m_lane, 0.0, level)

    occ_lane = lax.broadcasted_iota(jnp.int32, (16, 256), 1) // 32
    for g in range(2):
        row = jnp.zeros((16, 256), F32)
        for b in range(8):
            row = jnp.where(occ_lane == b, occ_ref[g * 8 + b].astype(F32), row)
        pooled[1 + g, pl.ds(64, 16), :] = row.astype(BF)

    for h in range(8):
        vals[h, pl.ds(64, 16), :] = jnp.ones((16, 2048), BF)
        qry[h, pl.ds(64 * (1 - h % 2), 64), :] = jnp.zeros((64, 1024), BF)

    loads["ghost"].wait()
    loads["pool"].wait()
    loads["lat"].wait()

    forwards = []
    for index, slot in ((0, 3), (1, 4)):
        part = store.at[pl.ds(slot * UNITS + core * HALF, HALF)]
        remote(part, part, 4 + index, index, me + 1 - 2 * core).wait_recv()
        forward = remote(part, part, 4 + index, 4 + index, me + 1 - 2 * core)
        forward.start()
        forwards.append(forward)

    gained_proj = (proj_tile.astype(F32) * gain_ref[...]).astype(BF)
    proj_k[...] = dot(gained_proj, qkv_w[1]).astype(BF)
    proj_v[...] = dot_nt(vw_t[...], gained_proj).astype(BF)
    proj_q[...] = dot_nt(qw_t[...], gained_proj).astype(BF)
    for half in range(2):
        tokens = pl.ds(half * 512, 512)
        latent = lat[pl.ds(512 + half * 512, 512), :]
        gained = (latent.astype(F32) * gain_ref[...]).astype(BF)
        lat_k[tokens, :] = dot(gained, qkv_w[1])
        lat_v[:, tokens] = dot_nt(vw_t[...], gained)
        lat_q[:, tokens] = dot_nt(qw_t[...], gained)
        base_t[:, tokens] = dot_nt(eye, latent)

    sends[2].wait_recv()
    sends[3].wait_recv()
    for index, slot in ((0, 3), (1, 4)):
        part = store.at[pl.ds(slot * UNITS + (1 - core) * HALF, HALF)]
        remote(part, part, 4 + index, 4 + index, me + 1 - 2 * core).wait_recv()

    lat_sends = [
        remote(lat.at[pl.ds(512, 512)], lat.at[pl.ds(1536, 512)], 6, 6, me - 1),
        remote(lat.at[pl.ds(1024, 512)], lat.at[pl.ds(0, 512)], 7, 7, me + 1),
    ]
    for copy in lat_sends:
        copy.start()

    lane = lax.broadcasted_iota(jnp.int32, (32, 128), 1)
    low_x = lane < 64
    low_y = (lane // 8 % 8 == 7, lane < 48)
    low_z = ((lane % 8 == 7), ((lane < 96) & (lane % 8 == 7)) | ((lane >= 96) & (lane < 112)))
    third = lane // 40
    first_extra = lane % 40 < 20

    def pick(b, carry):
        rows = pl.ds(b * 32, 32)
        tiles = []
        for face in range(6):
            peer = nbr_ref[face, b]
            rel = peer // 16 - 2 * chip
            slot = jnp.where(
                rel == 0, 0, jnp.where(rel == 1, 1, jnp.where(rel == -1, 3, jnp.where(rel == 2, 4, 2)))
            )
            start = jnp.where(peer >= 0, slot, 5) * UNITS
            brick = jnp.where(peer >= 0, peer % 16, 0)
            own_third = jnp.where(brick >= 12, 2, jnp.where(brick >= 6, 1, 0))
            found = [store[start + brick]]
            if face >= 2:
                found.append(store[start + 16 + brick])
            if face >= 4:
                extra = store[start + 32 + brick - 6 * own_third]
                mine = (third == own_third) & (first_extra if face == 4 else jnp.logical_not(first_extra))
                found.append(jnp.where(mine, extra, jnp.zeros_like(extra)))
            tiles.append(found)
        picked = [jnp.where(low_y[t], tiles[2][t], tiles[3][t]) for t in range(2)]
        picked.append(jnp.where(low_x, tiles[0][0], tiles[1][0]))
        picked += [jnp.where(low_z[t], tiles[4][t], tiles[5][t]) for t in range(2)]
        picked.append(tiles[4][2] + tiles[5][2])
        for index, tile in enumerate(picked):
            ghosts[rows, pl.ds(index * 128, 128)] = tile
        return carry

    lax.fori_loop(0, 16, pick, 0)

    inner = pl.ds(1, 4)
    for g in range(2):
        rows = pl.ds(g * 256, 256)

        def ghost_part(start, count, lanes):
            return dot_nt(ghost_t[pl.ds(start, count), lanes], ghosts[rows, lanes]).astype(BF)

        for index, i in enumerate((0, 3)):
            part = ghost_part(index * 256, 256, pl.ds(256, 128)).reshape(4, 4, 16, 256)
            slabs[g, i, inner, inner] = slabs[g, i, inner, inner] + part
        for index, j in enumerate((0, 5)):
            part = ghost_part(512 + index * 384, 384, pl.ds(0, 768)).reshape(4, 6, 16, 256)
            slabs[g, :, j] = slabs[g, :, j] + part
        for index, k in enumerate((0, 5)):
            part = ghost_part(1280 + index * 256, 256, pl.ds(256, 512)).reshape(4, 4, 16, 256)
            slabs[g, :, inner, k] = slabs[g, :, inner, k] + part

    def conv_group(g, carry):
        total = jnp.zeros((256, 512), F32)
        for tap in range(27):
            i, j, k = tap // 9, tap // 3 % 3, tap % 3
            patch = slabs[g, pl.ds(i, 2), pl.ds(j, 4), pl.ds(k, 4)].reshape(512, 256)
            total = total + dot_nt(block_w[tap], patch)
        rows = pl.ds(pl.multiple_of(g * 256, 256), 256)
        conv_s[rows, :] = total
        return carry

    lax.fori_loop(0, 2, conv_group, 0)
    for g in range(2):
        parts = []
        for b in range(8):
            rows = pl.ds(g * 256 + b * 32, 32)
            pre = conv_s[rows, :] + bias_col
            mixed = masked_s[rows, :].astype(F32) + pre / (1.0 + jnp.exp(-pre))
            parts.append(jnp.where(occ_ref[g * 8 + b] > 0, mixed, 0.0).astype(BF))
        conv_g = jnp.concatenate(parts, axis=0)
        pooled[1 + g, pl.ds(0, 64), :] = dot_nt(pool_t[...], conv_g).astype(BF)
        masked_s[pl.ds(g * 256, 256), :] = conv_g

    pool_sends = [
        remote(pooled.at[1], pooled.at[3], 8, 8, me - 1),
        remote(pooled.at[2], pooled.at[0], 9, 9, me + 1),
    ]
    for copy in pool_sends:
        copy.start()
    conv_out_ref[...] = dot(masked_s[...], order_t[...]).astype(BF)

    wide_row = lax.broadcasted_iota(jnp.int32, (512, 256), 0)
    wide_lane = lax.broadcasted_iota(jnp.int32, (512, 256), 1)
    same_brick = wide_row // 64 == wide_lane // 32
    first_lane = same_brick & (wide_lane % 32 == 0)
    def project(g):
        cells = pooled[g, pl.ds(0, 64), :]
        tall = jnp.concatenate([cells] * 8, axis=0)
        tall = jnp.where(same_brick, tall, jnp.zeros_like(tall))
        latent = lat[pl.ds(g * 512, 512), :]
        mixed = latent.astype(F32) + dot(tall, proj_tile)
        scale = lax.rsqrt(jnp.mean(mixed * mixed, axis=-1, keepdims=True) + 1e-06)
        if g in (1, 2):
            lanes = pl.ds((g - 1) * 512, 512)
            whole = base_t[:, lanes] + dot_nt(proj_t[...], tall)
            base_t[:, lanes] = whole
            scale_row = lax.rsqrt(jnp.mean(whole * whole, axis=0, keepdims=True) + 1e-06)
            k_all = ((lat_k[lanes, :] + dot(tall, proj_k[...])) * scale).astype(BF)
            v_all = ((lat_v[:, lanes] + dot_nt(proj_v[...], tall)) * scale_row).astype(BF)
            q_all = ((lat_q[:, lanes] + dot_nt(proj_q[...], tall)) * (scale_row * Q_SCALE)).astype(BF)
            for h in range(8):
                qry[h, pl.ds(64 * (h % 2), 64), lanes] = q_all[h * 64 : h * 64 + 64]
        else:
            normed = (mixed * scale * gain_ref[...]).astype(BF)
            k_all = dot(normed, qkv_w[1]).astype(BF)
            v_all = dot_nt(vw_t[...], normed).astype(BF)
            alive = jnp.broadcast_to(pooled[g, pl.ds(64, 16), :][:1], (128, 256))
            level = dot_nt(first_lane.astype(F32).astype(BF), alive)
            level = jnp.where(level > 0.5, 0.0, NEG)
            mask[1, g // 3] = jnp.concatenate([level] * 4, axis=1)
        for pair in range(4):
            keys[pair, pl.ds(g * 512, 512), :] = k_all[:, pair * 128 : pair * 128 + 128]
        for h in range(8):
            vals[h, pl.ds(0, 64), pl.ds(g * 512, 512)] = v_all[h * 64 : h * 64 + 64]

    def score_chunk(side, half, pair, h, chunk, dst):
        rows = pl.ds(chunk * 256, 256)
        base = 512 + half * 512 if side == 0 else half * 1536
        part = dot(keys[pair, pl.ds(base + chunk * 256, 256), :], qry[h, :, pl.ds(half * 512, 512)])
        part = part + mask[side, half, rows, :]
        dst[rows, :] = part
        return jnp.max(part.reshape(32, 8, 512), axis=0)

    def head_step(side, half, h, now, peaks, nxt, n_half, n_pair, n_head):
        lanes = pl.ds(half * 512, 512)
        base = 512 + half * 512 if side == 0 else half * 1536
        peak = jnp.max(peaks, axis=0, keepdims=True)
        if side == 1:
            own_peak = parts_s[h, pl.ds(72, 8), lanes][:1]
            peak = jnp.maximum(peak, own_peak)
        new_peaks, total = None, None
        for chunk in range(2):
            if nxt is not None:
                top = score_chunk(side, n_half, n_pair, n_head, chunk, nxt)
                new_peaks = top if chunk == 0 else jnp.maximum(new_peaks, top)
            weights = jnp.exp2(now[pl.ds(chunk * 256, 256), :] - peak).astype(BF)
            part = dot(vals[h, :, pl.ds(base + chunk * 256, 256)], weights)
            total = part if chunk == 0 else total + part
        if side == 0:
            parts_s[h, pl.ds(0, 72), lanes] = total[:72]
            parts_s[h, pl.ds(72, 8), lanes] = jnp.broadcast_to(peak, (8, 512))
        else:
            total = total[:72] + parts_s[h, pl.ds(0, 72), lanes] * jnp.exp2(own_peak - peak)
            out = (total[:64] / total[64:65]).astype(BF)
            att[pl.ds(pl.multiple_of(h * 64, 64), 64), lanes] = out
        return new_peaks

    def attend(side):
        peaks = None
        for chunk in range(2):
            top = score_chunk(side, 0, 0, 0, chunk, even_s)
            peaks = top if chunk == 0 else jnp.maximum(peaks, top)
        for half in range(2):

            def pair_step(pair, tops):
                tops = head_step(side, half, pair * 2, even_s, tops, odd_s, half, pair, pair * 2 + 1)
                return head_step(side, half, pair * 2 + 1, odd_s, tops, even_s, half, pair + 1, pair * 2 + 2)

            peaks = lax.fori_loop(0, 3, pair_step, peaks)
            peaks = head_step(side, half, 6, even_s, peaks, odd_s, half, 3, 7)
            peaks = head_step(side, half, 7, odd_s, peaks, even_s if half == 0 else None, 1, 0, 0)
            if side == 1:
                lanes = pl.ds(half * 512, 512)
                tokens_ref[:, lanes] = (base_t[:, lanes] + dot(ow_t[...], att[:, lanes])).astype(BF)

    project(1)
    project(2)
    attend(0)
    for copy in lat_sends + pool_sends:
        copy.wait_recv()
    project(0)
    project(3)
    attend(1)

    for copy in sends + forwards + lat_sends + pool_sends:
        copy.wait_send()


def local(n_space, n_chan, features, occupancy, neighbours, conv_weight, conv_bias, latent, token_proj, norm_gain, qkv_weight, out_weight):
    tables = slab_tables()
    smem = pl.BlockSpec(memory_space=pltpu.SMEM)
    vmem = pl.BlockSpec(memory_space=pltpu.VMEM)
    hbm = pl.BlockSpec(memory_space=pl.ANY)
    conv_out, tokens_out = pl.pallas_call(
        functools.partial(kernel, n_space, n_chan),
        out_shape=(pltpu.VMEM((512, 512), BF), pltpu.VMEM((512, 1024), BF)),
        in_specs=[smem, smem, vmem, vmem, vmem] + [hbm] * 11,
        out_specs=(vmem, vmem),
        scratch_shapes=[
            pltpu.VMEM((512, 512), BF),
            pltpu.VMEM((27, 32, 32), BF),
            pltpu.VMEM((2048, 512), BF),
            pltpu.VMEM((3, 512, 512), BF),
            pltpu.VMEM((512, 512), BF),
            pltpu.VMEM((ROWS, 512), BF),
            pltpu.VMEM((GHOST_ROWS, 768), BF),
            pltpu.VMEM((512, 256), BF),
            pltpu.VMEM((3, 512, 128), BF),
            pltpu.VMEM((512, 512), BF),
            pltpu.VMEM((64, 512), BF),
            pltpu.VMEM((6 * UNITS, 32, 128), BF),
            pltpu.VMEM((512, 768), BF),
            pltpu.VMEM((2,) + SLABS + (16, 256), BF),
            pltpu.VMEM((27, 256, 256), BF),
            pltpu.VMEM((512, 512), BF),
            pltpu.VMEM((512, 512), F32),
            pltpu.VMEM((4, 80, 256), BF),
            pltpu.VMEM((512, 256), BF),
            pltpu.VMEM((512, 512), BF),
            pltpu.VMEM((512, 512), BF),
            pltpu.VMEM((512, 512), BF),
            pltpu.VMEM((512, 1024), F32),
            pltpu.VMEM((2, 2, 512, 512), F32),
            pltpu.VMEM((4, 2048, 128), BF),
            pltpu.VMEM((8, 80, 2048), BF),
            pltpu.VMEM((8, 128, 1024), BF),
            pltpu.VMEM((512, 1024), BF),
            pltpu.VMEM((512, 512), F32),
            pltpu.VMEM((512, 512), F32),
            pltpu.VMEM((8, 80, 1024), F32),
            pltpu.VMEM((1024, 512), F32),
            pltpu.VMEM((512, 1024), F32),
            pltpu.VMEM((512, 1024), F32),
            pltpu.VMEM((256, 512), BF),
            pltpu.VMEM((512, 256), BF),
            pltpu.VMEM((512, 256), BF),
            pltpu.SemaphoreType.DMA((11,)),
            pltpu.SemaphoreType.DMA((10,)),
            pltpu.SemaphoreType.DMA((10,)),
        ],
        compiler_params=pltpu.CompilerParams(
            collective_id=0, has_side_effects=True, vmem_limit_bytes=60 * 1024 * 1024
        ),
        cost_estimate=pl.CostEstimate(flops=8 * 10**9, bytes_accessed=12 * 10**6, transcendentals=9 * 10**6),
    )(
        occupancy,
        neighbours.T,
        conv_bias.reshape(1, 32),
        norm_gain.reshape(1, 512),
        token_proj,
        features.reshape(512, 512),
        conv_weight,
        latent,
        qkv_weight,
        out_weight,
        *tables,
    )
    return conv_out.reshape(16, 32, 512), tokens_out


def solution(mesh):
    both = ("space", "chan")
    return jax.shard_map(
        functools.partial(local, mesh.shape["space"], mesh.shape["chan"]),
        mesh=mesh,
        in_specs=(
            P(both, None, None),
            P(both),
            P(both, None),
            P(),
            P(),
            P(both, None),
            P(),
            P(),
            P(),
            P(),
        ),
        out_specs=(P(both, None, None), P(None, both)),
        check_vma=False,
    )
```
